32 devices in a mesh: stream: 4 (over y, x), cross: 8 (over z, core).
Axes of the slice: x: 2, y: 2, z: 4, core: 2. Of those that a mesh axis runs over, the one named last changes fastest.
Arguments:
- velocity: bfloat16 [128, 3, 48, 64, 128], P(None, None, 'stream', 'cross'), may hold values from -40 to 40, as said below
- metric_x: float32 [48], P('stream'), may hold values from 0.5 to 2
- metric_y: float32 [64], P('cross'), may hold values from 0.5 to 2
- metric_z: float32 [128], replicated, may hold values from 0.5 to 2
Outputs:
- modes: bfloat16 [128, 4, 48, 64, 128], P(None, None, 'stream', 'cross')
- factor: float32 [128, 128], replicated
The draws below stay inside these ranges and needn't reach their ends.
Inputs may be any that keep to these rules, and one draw needn't show every extreme that they name: velocity snapshots share a common part across snapshots.
All inputs are finite; a program needn't handle non-finite values.
Results may differ from the reference program's by a relative error of at most 0.0023.
The reference program's roundings to bfloat16 on the way count: a program that leaves them out, or rounds other values in their place, can miss the bound.
Values may be sent and summed in bfloat16 or wider, within the bound.
No kernel may reach another device: no remote copies, remote signals or barrier semaphores. Data moves between devices by JAX's collectives and lax.ppermute only.
A program may use at most 128 MiB of HBM per device.

```python
import math
import jax
import jax.numpy as jnp
from jax import lax

SNAP = 128
NZ = 128
NX = 48
NY = 64


def draw_velocity(key, part):
    key_noise, key_common, key_rough = jax.random.split(jax.random.fold_in(key, 17), 3)
    shape = (SNAP, 3, NX, NY, NZ)
    common_shape = (1, 3, NX, NY, NZ)
    noise = jax.random.normal(key_noise, shape, jnp.float32)
    common = jax.random.normal(key_common, common_shape, jnp.float32)
    weight = 1.5
    rough = 2.0 ** jax.random.uniform(key_rough, common_shape, jnp.float32, -1.0, 1.0)
    rising = 10.0 ** (0.8 * jnp.arange(NY, dtype=jnp.float32) / NY)
    value = (weight * common + 0.5 * noise * rising[None, None, None, :, None]) * rough
    return jnp.clip(value, -40.0, 40.0).astype(jnp.bfloat16)


def levels(rng, extent, shards, least, top_value):
    def one(dim, blocks):
        draws = jax.random.uniform(jax.random.fold_in(jax.random.fold_in(rng, 6), dim), (blocks,), jnp.float32, least / len(shards), top_value / len(shards))
        return jnp.repeat(jnp.exp(draws), extent[dim] // blocks).reshape((-1,) + (1,) * (len(extent) - dim - 1))

    gain = one(*shards[0])
    for cut in shards[1:]:
        gain = gain * one(*cut)
    return gain


def setup_inputs(seed: int = 0) -> dict:
    seeds = jax.random.split(jax.random.key(seed), 5)
    return {
        "velocity": draw_velocity(jax.random.fold_in(seeds[4], 71), 0),
        "metric_x": jnp.clip(jnp.exp(math.log(2.0) - 1.3862944 * jax.random.uniform(seeds[1], (NX,), jnp.float32) ** levels(seeds[1], (NX,), ((0, 4),), -0.2, 0.2)), 0.5, 2.0),
        "metric_y": jnp.clip(jnp.exp(math.log(2.0) - 1.3862944 * jax.random.uniform(seeds[2], (NY,), jnp.float32) ** levels(seeds[2], (NY,), ((0, 8),), -0.2, 0.2)), 0.5, 2.0),
        "metric_z": jnp.clip(jnp.exp(jax.random.uniform(seeds[3], (NZ,), jnp.float32, math.log(0.5), math.log(2.0))), 0.5, 2.0),
    }


def central(padded, axis):
    count = padded.shape[axis] - 4

    def part_at(offset):
        return lax.slice_in_dim(padded, offset, offset + count, axis=axis)
    return (8.0 * (part_at(3) - part_at(1)) - (part_at(4) - part_at(0))) / 12.0

def fields(block, metric_x, metric_y, metric_z):
    values = block.astype(jnp.float32)

    def deriv_x(field):
        return central(field[:, :, 2:-2, :], 1) * metric_x[:, None, None]

    def deriv_y(field):
        return central(field[:, 2:-2, :, :], 2) * metric_y[:, None]

    def deriv_z(field):
        interior = field[:, 2:-2, 2:-2, :]
        return central(jnp.pad(interior, ((0, 0), (0, 0), (0, 0), (2, 2))), 3) * metric_z
    stream_vel = values[:, 0]
    cross_vel = values[:, 1]
    span_vel = values[:, 2]
    vort_x = deriv_y(span_vel) - deriv_z(cross_vel)
    vort_y = deriv_z(stream_vel) - deriv_x(span_vel)
    vort_z = deriv_x(cross_vel) - deriv_y(stream_vel)
    dilatation = deriv_x(stream_vel) + deriv_y(cross_vel) + deriv_z(span_vel)
    return jnp.stack([vort_x, vort_y, vort_z, dilatation], axis=1).astype(jnp.bfloat16)

def inner_products(flat):
    return lax.dot_general(flat.astype(jnp.float32), flat.astype(jnp.float32), (((1,), (1,)), ((), ())), preferred_element_type=jnp.float32)

def reference(velocity, metric_x, metric_y, metric_z):
    blocks = velocity.reshape(SNAP // 8, 8, 3, NX, NY, NZ)

    def one_block(block):
        padded = jnp.pad(block, ((0, 0), (0, 0), (2, 2), (2, 2), (0, 0)))
        return fields(padded, metric_x, metric_y, metric_z)
    flat = lax.map(one_block, blocks).reshape(SNAP, 4 * NX * NY * NZ)
    scale = 1.0 / (4.0 * NX * NY * NZ)
    gram = inner_products(flat) * scale
    lower = jnp.linalg.cholesky(gram)
    identity = jnp.eye(SNAP, dtype=jnp.float32)
    inverse = jax.scipy.linalg.solve_triangular(lower, identity, lower=True)
    basis = jnp.dot(inverse.astype(jnp.bfloat16).astype(jnp.float32), flat.astype(jnp.float32), preferred_element_type=jnp.float32).astype(jnp.bfloat16)
    return (basis.reshape(SNAP, 4, NX, NY, NZ), lower)
```

```python
import functools

import jax
import jax.numpy as jnp
from jax import lax
from jax.experimental import pallas as pl
from jax.experimental.pallas import tpu as pltpu
from jax.sharding import PartitionSpec as P

F32, BF16 = jnp.float32, jnp.bfloat16
VMEM_LIMIT = 56 * 1024 * 1024


def params():
    return pltpu.CompilerParams(vmem_limit_bytes=VMEM_LIMIT)


def planes_kernel(cells_ref, out_ref, rows):
    snaps, _, layers, cells_y, cells_z = cells_ref.shape
    for layer in range(layers):
        rows[...] = cells_ref[:, 0, layer].astype(F32).reshape(snaps * cells_y, cells_z)
        for y in range(cells_y):
            out_ref[0, layer, y] = rows[pl.ds(y, snaps, stride=cells_y), :].astype(BF16)


def planes(velocity, picks, width):
    snaps, comps, _, cells_y, cells_z = velocity.shape
    first, count, step = picks
    return pl.pallas_call(
        planes_kernel,
        grid=(comps, count),
        in_specs=[
            pl.BlockSpec(
                (snaps, 1, width, cells_y, cells_z), lambda c, i: (0, c, first + step * i, 0, 0)
            )
        ],
        out_specs=pl.BlockSpec(
            (1, width, cells_y, snaps, cells_z), lambda c, i: (c, i, 0, 0, 0)
        ),
        out_shape=jax.ShapeDtypeStruct((comps, count * width, cells_y, snaps, cells_z), BF16),
        scratch_shapes=[pltpu.VMEM((snaps * cells_y, cells_z), F32)],
        compiler_params=params(),
    )(velocity)


ROWS = 16


def layer_fields(ring, slots, rz, low, high, metric_x, metric_y_ref, metric_z, out_ref):
    cells_y, snaps, cells_z = ring.shape[2:]
    back2, back1, here, fore1, fore2 = slots

    def some_rows(step, _):
        at = pl.ds(pl.multiple_of(step * ROWS, ROWS), ROWS)

        def row(comp, y):
            if y < 0:
                return low[comp, 0, y + 2, at, :].astype(F32)
            if y >= cells_y:
                return high[comp, 0, y - cells_y, at, :].astype(F32)
            return ring[here, comp, y, at, :]

        window = [[row(c, y) for y in range(-2, 2)] for c in range(3)]
        for y in range(cells_y):
            for c in range(3):
                window[c].append(row(c, y + 2))

            def along_x(c):
                near = ring[fore1, c, y, at, :] - ring[back1, c, y, at, :]
                far = ring[fore2, c, y, at, :] - ring[back2, c, y, at, :]
                return (8.0 * near - far) * metric_x

            def along_y(c):
                w = window[c]
                return (8.0 * (w[3] - w[1]) - (w[4] - w[0])) * metric_y_ref[y]

            def along_z(c):
                return rz[c, y, at, :] * metric_z

            outs = (
                along_y(2) - along_z(1),
                along_z(0) - along_x(2),
                along_x(1) - along_y(0),
                along_x(0) + along_y(1) + along_z(2),
            )
            for f, value in enumerate(outs):
                lane = (f * cells_y + y) * cells_z
                out_ref[0, at, lane : lane + cells_z] = value.astype(BF16)
            for c in range(3):
                window[c] = window[c][1:]
        return 0

    lax.fori_loop(0, snaps // ROWS, some_rows, 0)


def fields_kernel(span, pick, n_layers, mx_ref, my_ref, mz_ref, taps_ref, *rest):
    layer_refs = rest[:n_layers]
    low_ref, high_ref, out_ref, gram_ref, ring, rz_ring = rest[n_layers:]
    i = pl.program_id(0)
    j = lax.rem(i, span)
    cells_y, snaps, cells_z = ring.shape[2:]

    @pl.when(i == 0)
    def _():
        gram_ref[...] = jnp.zeros_like(gram_ref)

    def take(ref):
        block = ref[:, 0]
        ring[lax.rem(j, 5)] = block.astype(F32)

        @pl.when((j >= 2) & (j < span - 2))
        def _():
            flat = block.reshape(3 * cells_y * snaps, cells_z)
            rz_ring[lax.rem(j, 3)] = jnp.dot(
                flat, taps_ref[...], preferred_element_type=F32
            ).reshape(3, cells_y, snaps, cells_z)

    which = pick(i)
    for k, ref in enumerate(layer_refs):
        pl.when(which == k)(functools.partial(take, ref))

    @pl.when(j >= 4)
    def _():
        slots = [lax.rem(j + 1 + k, 5) for k in range(5)]
        layer_fields(
            ring,
            slots,
            rz_ring.at[lax.rem(j - 2, 3)],
            low_ref,
            high_ref,
            mx_ref[i],
            my_ref,
            mz_ref[...],
            out_ref,
        )
        done = out_ref[0]
        gram_ref[...] += lax.dot_general(
            done, done, (((1,), (1,)), ((), ())), preferred_element_type=F32
        )


def fields(sources, pick, maps, segments, span, center, low, high, metric_x, metric_y, metric_z):
    comps, _, cells_y, snaps, cells_z = sources[0].shape
    taps = jnp.zeros((cells_z, cells_z), F32)
    for shift, weight in ((1, 8.0), (-1, -8.0), (2, -1.0), (-2, 1.0)):
        taps = taps + weight * jnp.eye(cells_z, k=-shift, dtype=F32)
    steps = segments * span
    lanes = 4 * cells_y * cells_z
    kept = span - 4

    def out_index(i):
        return (i // span) * kept + jnp.maximum(lax.rem(i, span) - 4, 0)

    halo_spec = pl.BlockSpec((comps, 1, 2, snaps, cells_z), lambda i: (0, center(i), 0, 0, 0))
    return pl.pallas_call(
        functools.partial(fields_kernel, span, pick, len(sources)),
        grid=(steps,),
        in_specs=[
            pl.BlockSpec(memory_space=pltpu.SMEM),
            pl.BlockSpec(memory_space=pltpu.SMEM),
            pl.BlockSpec((1, cells_z), lambda i: (0, 0)),
            pl.BlockSpec((cells_z, cells_z), lambda i: (0, 0)),
        ]
        + [
            pl.BlockSpec(
                (comps, 1, cells_y, snaps, cells_z),
                functools.partial(lambda m, i: (0, m(i), 0, 0, 0), m),
            )
            for m in maps
        ]
        + [halo_spec, halo_spec],
        out_specs=[
            pl.BlockSpec((1, snaps, lanes), lambda i: (out_index(i), 0, 0)),
            pl.BlockSpec((snaps, snaps), lambda i: (0, 0)),
        ],
        out_shape=[
            jax.ShapeDtypeStruct((segments * kept, snaps, lanes), BF16),
            jax.ShapeDtypeStruct((snaps, snaps), F32),
        ],
        scratch_shapes=[
            pltpu.VMEM((5, comps, cells_y, snaps, cells_z), F32),
            pltpu.VMEM((3, comps, cells_y, snaps, cells_z), F32),
        ],
        compiler_params=params(),
    )(
        metric_x[jnp.array([center(i) for i in range(steps)])] / 12.0,
        metric_y / 12.0,
        metric_z[None, :] / 12.0,
        taps.astype(BF16),
        *sources,
        low,
        high,
    )


def modes_kernel(pick, n_sources, inverse_ref, *rest):
    sources, (out_ref, rows) = rest[:n_sources], rest[n_sources:]
    snaps, comps, _, cells_y, cells_z = out_ref.shape
    width = cells_y * cells_z
    which = pick(pl.program_id(0))

    def take(ref):
        for f in range(comps):
            whole = jnp.dot(
                inverse_ref[...], ref[0, :, f * width : (f + 1) * width], preferred_element_type=F32
            )
            for y in range(cells_y):
                rows[pl.ds(y, snaps, stride=cells_y), :] = whole[:, y * cells_z : (y + 1) * cells_z]
            out_ref[:, f, 0] = rows[...].reshape(snaps, cells_y, cells_z).astype(BF16)

    for k, ref in enumerate(sources):
        pl.when(which == k)(functools.partial(take, ref))


def modes(inverse, sources, pick, maps, cells_x, cells_y, cells_z):
    snaps = inverse.shape[0]
    lanes = sources[0].shape[2]
    return pl.pallas_call(
        functools.partial(modes_kernel, pick, len(sources)),
        grid=(cells_x,),
        in_specs=[pl.BlockSpec((snaps, snaps), lambda i: (0, 0))]
        + [
            pl.BlockSpec((1, snaps, lanes), functools.partial(lambda m, i: (m(i), 0, 0), m))
            for m in maps
        ],
        out_specs=pl.BlockSpec((snaps, 4, 1, cells_y, cells_z), lambda i: (0, 0, i, 0, 0)),
        out_shape=jax.ShapeDtypeStruct((snaps, 4, cells_x, cells_y, cells_z), BF16),
        scratch_shapes=[pltpu.VMEM((snaps * cells_y, cells_z), F32)],
        compiler_params=params(),
    )(inverse, *sources)


def total(local):
    for axis in ("cross", "stream"):
        count = lax.axis_size(axis)
        if count & (count - 1):
            local = lax.psum(local, axis)
            continue
        step = 1
        while step < count:
            local = local + lax.ppermute(local, axis, [(i, i ^ step) for i in range(count)])
            step *= 2
    return local


def shift(cells, axis, way):
    count = lax.axis_size(axis)
    pairs = [(i, i + way) for i in range(count) if 0 <= i + way < count]
    return lax.ppermute(cells, axis, pairs)


def shards(velocity, metric_x, metric_y, metric_z):
    snaps, comps, cells_x, cells_y, cells_z = velocity.shape
    edges = planes(velocity, (0, 2, cells_x // 2 - 1), 2)
    before = shift(edges[:, 2:], "stream", 1)
    after = shift(edges[:, :2], "stream", -1)
    cells = planes(velocity, (0, cells_x // 2, 1), 2)
    low = shift(cells[:, :, cells_y - 2 :], "cross", 1)
    high = shift(cells[:, :, :2], "cross", -1)

    inner, inner_gram = fields(
        [cells],
        lambda i: 0,
        [lambda i: i],
        1,
        cells_x,
        lambda i: jnp.clip(i - 2, 0, cells_x - 1),
        low,
        high,
        metric_x,
        metric_y,
        metric_z,
    )
    outer, outer_gram = fields(
        [before, cells, after],
        lambda i: jnp.where(i < 2, 0, jnp.where(i < 10, 1, 2)),
        [
            lambda i: jnp.minimum(i, 1),
            lambda i: jnp.where(i < 6, jnp.maximum(i - 2, 0), jnp.minimum(i - 6 + cells_x - 4, cells_x - 1)),
            lambda i: jnp.maximum(i - 10, 0),
        ],
        2,
        6,
        lambda i: jnp.where(i < 6, jnp.maximum(i - 4, 0), jnp.maximum(i - 10, 0) + cells_x - 2),
        low,
        high,
        metric_x,
        metric_y,
        metric_z,
    )
    everywhere = (
        4.0 * cells_x * lax.axis_size("stream") * cells_y * lax.axis_size("cross") * cells_z
    )
    gram = total(inner_gram + outer_gram)
    lower = jnp.linalg.cholesky(gram * (1.0 / everywhere))
    inverse = jax.scipy.linalg.solve_triangular(lower, jnp.eye(snaps, dtype=F32), lower=True)
    basis = modes(
        inverse.astype(BF16),
        [inner, outer],
        lambda i: jnp.where((i >= 2) & (i < cells_x - 2), 0, 1),
        [
            lambda i: jnp.clip(i - 2, 0, cells_x - 5),
            lambda i: jnp.where(i < cells_x - 2, jnp.minimum(i, 1), i - (cells_x - 4)),
        ],
        cells_x,
        cells_y,
        cells_z,
    )
    return basis, lower


def solution(mesh):
    return jax.shard_map(
        shards,
        mesh=mesh,
        in_specs=(P(None, None, "stream", "cross", None), P("stream"), P("cross"), P()),
        out_specs=(P(None, None, "stream", "cross", None), P()),
        check_vma=False,
    )
```

```python
import functools

import jax
import jax.numpy as jnp
from jax import lax
from jax.experimental import pallas as pl
from jax.experimental.pallas import tpu as pltpu
from jax.sharding import PartitionSpec as P

F32, BF16 = jnp.float32, jnp.bfloat16
VMEM_LIMIT = 56 * 1024 * 1024
PITCH = 9
ROWS = 16
HBM = pl.BlockSpec(memory_space=pl.ANY)
SMEM = pl.BlockSpec(memory_space=pltpu.SMEM)
VMEM = pl.BlockSpec(memory_space=pltpu.VMEM)
PARAMS = pltpu.CompilerParams(vmem_limit_bytes=VMEM_LIMIT)
SHORT = pl.CostEstimate(flops=1024, bytes_accessed=1024, transcendentals=0)
DMA = pltpu.SemaphoreType.DMA


def turn(tile, rows, ys, put):
    snaps, cells_y, cells_z = tile.shape
    wide = tile.astype(F32)
    for s in range(snaps):
        rows[pl.ds(s * PITCH, cells_y), :] = wide[s]
    for y in ys:
        put(y, rows[pl.ds(y, snaps, stride=PITCH), :].astype(BF16))


def edges_kernel(
    velocity, near, far1, far2, first, last, tiles, inner, ends, sides, rows, *sems
):
    end_in, inner_in, end_out, side_out = sems
    snaps, comps, cells_x, cells_y, _ = velocity.shape
    odd = lax.rem(lax.axis_index("stream"), 2)
    firsts = ((1 - odd) * (cells_x - 2), odd * (cells_x - 2))
    half = cells_y // 2
    between = cells_x - 4
    order = [(side, c) for side in (1, 0) for c in range(comps)]

    def end_read(side, c):
        return pltpu.make_async_copy(
            velocity.at[:, c, pl.ds(firsts[side], 2)], tiles.at[side, c], end_in.at[side, c]
        )

    def inner_read(c):
        return pltpu.make_async_copy(
            velocity.at[:, c, pl.ds(2, between)], inner.at[c], inner_in.at[c]
        )

    def side_writes(c, x):
        return [
            pltpu.make_async_copy(sides.at[k, c, x], ref.at[c, x], side_out.at[k, c, x])
            for k, ref in enumerate((first, last))
        ]

    def put_side(c, x, y, plane):
        if y < 2:
            sides[0, c, x, y] = plane
        elif y >= cells_y - 2:
            sides[1, c, x, y - cells_y + 2] = plane

    for side, c in order:
        end_read(side, c).start()
    for c in range(comps):
        inner_read(c).start()
    writes = []
    for side, c in order:
        end_read(side, c).wait()

        def one_end(layer, _):
            x = firsts[side] + layer

            def put(y, plane):
                ends[side, c, layer, y] = plane
                put_side(c, x, y, plane)

            turn(tiles[side, c, :, layer], rows, range(cells_y), put)
            for w in side_writes(c, x):
                w.start()
            return 0

        lax.fori_loop(0, 2, one_end, 0)
        if side == 0:
            parts = [(ends.at[0, c], near.at[c])]
        else:
            parts = [
                (ends.at[1, c, :, pl.ds(0, half)], far1.at[c]),
                (ends.at[1, c, :, pl.ds(half, half)], far2.at[c]),
            ]
        for src, dst in parts:
            writes.append(pltpu.make_async_copy(src, dst, end_out.at[len(writes)]))
            writes[-1].start()

    for c in range(comps):
        inner_read(c).wait()

        def one_inner(n, _):
            turn(
                inner[c, :, n],
                rows,
                (0, 1, cells_y - 2, cells_y - 1),
                functools.partial(put_side, c, n + 2),
            )
            for w in side_writes(c, n + 2):
                w.start()
            return 0

        lax.fori_loop(0, between, one_inner, 0)

    for w in writes:
        w.wait()

    def finish(n, _):
        for w in side_writes(n // cells_x, lax.rem(n, cells_x)):
            w.wait()
        return 0

    lax.fori_loop(0, comps * cells_x, finish, 0)


def edges(velocity):
    snaps, comps, cells_x, cells_y, cells_z = velocity.shape
    shape = lambda layers, rows: jax.ShapeDtypeStruct((comps, layers, rows, snaps, cells_z), BF16)
    return pl.pallas_call(
        edges_kernel,
        in_specs=[HBM],
        out_specs=[HBM] * 5,
        out_shape=[shape(2, cells_y)] + [shape(2, cells_y // 2)] * 2 + [shape(cells_x, 2)] * 2,
        scratch_shapes=[
            pltpu.VMEM((2, comps, snaps, 2, cells_y, cells_z), BF16),
            pltpu.VMEM((comps, snaps, cells_x - 4, cells_y, cells_z), BF16),
            pltpu.VMEM((2, comps, 2, cells_y, snaps, cells_z), BF16),
            pltpu.VMEM((2, comps, cells_x, 2, snaps, cells_z), BF16),
            pltpu.VMEM((snaps * PITCH, cells_z), F32),
            DMA((2, comps)),
            DMA((comps,)),
            DMA((3 * comps,)),
            DMA((2, comps, cells_x)),
        ],
        compiler_params=PARAMS,
    )(velocity)


def planes_kernel(velocity, cells, taken, turned, rows, in_sems, out_sems):
    snaps, comps, cells_x, cells_y, cells_z = velocity.shape

    def read(c, x):
        return pltpu.make_async_copy(velocity.at[:, c, x], taken.at[c, x], in_sems.at[c, x])

    def write(c, x):
        return pltpu.make_async_copy(turned.at[c, x], cells.at[c, x], out_sems.at[c, x])

    def each(work):
        def step(n, _):
            work(n // cells_x, lax.rem(n, cells_x))
            return 0

        lax.fori_loop(0, comps * cells_x, step, 0)

    def one(c, x):
        read(c, x).wait()

        def put(y, plane):
            turned[c, x, y] = plane

        turn(taken[c, x], rows, range(cells_y), put)
        write(c, x).start()

    each(lambda c, x: read(c, x).start())
    each(one)
    each(lambda c, x: write(c, x).wait())


def planes(velocity):
    snaps, comps, cells_x, cells_y, cells_z = velocity.shape
    return pl.pallas_call(
        planes_kernel,
        in_specs=[HBM],
        out_specs=HBM,
        out_shape=jax.ShapeDtypeStruct((comps, cells_x, cells_y, snaps, cells_z), BF16),
        scratch_shapes=[
            pltpu.VMEM((comps, cells_x, snaps, cells_y, cells_z), BF16),
            pltpu.VMEM((comps, cells_x, cells_y, snaps, cells_z), BF16),
            pltpu.VMEM((snaps * PITCH, cells_z), F32),
            DMA((comps, cells_x)),
            DMA((comps, cells_x)),
        ],
        compiler_params=PARAMS,
    )(velocity)


def layer_fields(ys, ring, slots, rz, low, high, metric_x, metric_y_ref, metric_z, out_ref):
    cells_y, snaps, cells_z = ring.shape[2:]
    back2, back1, here, fore1, fore2 = slots

    def some_rows(step, _):
        at = pl.ds(pl.multiple_of(step * ROWS, ROWS), ROWS)
        held = {}

        def row(comp, y):
            if (comp, y) not in held:
                if y < 0:
                    held[comp, y] = low[comp, y + 2, at, :].astype(F32)
                elif y >= cells_y:
                    held[comp, y] = high[comp, y - cells_y, at, :].astype(F32)
                else:
                    held[comp, y] = ring[here, comp, y, at, :]
            return held[comp, y]

        for n, y in enumerate(ys):

            def along_x(c):
                near = ring[fore1, c, y, at, :] - ring[back1, c, y, at, :]
                far = ring[fore2, c, y, at, :] - ring[back2, c, y, at, :]
                return (8.0 * near - far) * metric_x

            def along_y(c):
                near = row(c, y + 1) - row(c, y - 1)
                far = row(c, y + 2) - row(c, y - 2)
                return (8.0 * near - far) * metric_y_ref[y]

            def along_z(c):
                return rz[c, y, at, :] * metric_z

            outs = (
                along_y(2) - along_z(1),
                along_z(0) - along_x(2),
                along_x(1) - along_y(0),
                along_x(0) + along_y(1) + along_z(2),
            )
            for f, value in enumerate(outs):
                lane = (f * len(ys) + n) * cells_z
                out_ref[at, lane : lane + cells_z] = value.astype(BF16)
        return 0

    lax.fori_loop(0, snaps // ROWS, some_rows, 0)


def runs(ys):
    found = []
    for y in ys:
        if found and found[-1][1] == y:
            found[-1][1] = y + 1
        else:
            found.append([y, y + 1])
    return found


def fields_kernel(reads, centers, ys, mx_ref, my_ref, mz_ref, taps_ref, *rest):
    n = len(rest) - 12
    sources, (low, high, out, gram_ref) = rest[:n], rest[n : n + 4]
    layers, lows, highs, ring, rz_ring, done, in_sems, out_sems = rest[n + 4 :]
    comps, cells_y, snaps, cells_z = ring.shape[1:]
    steps = len(centers)
    kept = [i for i in range(steps) if centers[i] is not None]
    lowest, highest = min(ys) < 2, max(ys) >= cells_y - 2

    def whichever(i, start):
        for m, (src, rows, cond) in enumerate(reads[i](sources)):
            copy = pltpu.make_async_copy(src, layers.at[i, :, rows], in_sems.at[0, i, m])
            if cond is None:
                getattr(copy, "start" if start else "wait")()
            else:
                pl.when(cond)(copy.start if start else copy.wait)

    def sides(k):
        x = centers[kept[k]]
        copies = []
        if lowest:
            copies.append(pltpu.make_async_copy(low.at[:, x], lows.at[k], in_sems.at[1, k, 0]))
        if highest:
            copies.append(pltpu.make_async_copy(high.at[:, x], highs.at[k], in_sems.at[2, k, 0]))
        return copies

    for i in range(steps):
        whichever(i, True)
        if centers[i] is not None:
            for copy in sides(kept.index(i)):
                copy.start()

    gram_ref[...] = jnp.zeros_like(gram_ref)
    writes = []
    for i in range(steps):
        whichever(i, False)
        ring[i % 5] = layers[i].astype(F32)
        if i + 2 < steps and centers[i + 2] is not None:
            for a, b in runs(ys):
                flat = layers[i, :, a:b].reshape(comps * (b - a) * snaps, cells_z)
                rz_ring[i % 3, :, a:b] = jnp.dot(
                    flat, taps_ref[...], preferred_element_type=F32
                ).reshape(comps, b - a, snaps, cells_z)
        if centers[i] is None:
            continue
        k = kept.index(i)
        for copy in sides(k):
            copy.wait()
        layer_fields(
            ys,
            ring,
            [(i + 1 + s) % 5 for s in range(5)],
            rz_ring.at[(i - 2) % 3],
            lows.at[k],
            highs.at[k],
            mx_ref[centers[i]],
            my_ref,
            mz_ref[...],
            done.at[k],
        )
        writes.append(pltpu.make_async_copy(done.at[k], out.at[k], out_sems.at[k]))
        writes[-1].start()
        gram_ref[...] += lax.dot_general(
            done[k], done[k], (((1,), (1,)), ((), ())), preferred_element_type=F32
        )
    for w in writes:
        w.wait()


def fields(sources, reads, centers, ys, low, high, metrics):
    comps, _, cells_y, snaps, cells_z = sources[0].shape
    steps = len(centers)
    kept = sum(c is not None for c in centers)
    lanes = 4 * len(ys) * cells_z
    return pl.pallas_call(
        functools.partial(fields_kernel, reads, centers, ys),
        in_specs=[SMEM, SMEM, VMEM, VMEM] + [HBM] * (len(sources) + 2),
        out_specs=[HBM, VMEM],
        out_shape=[
            jax.ShapeDtypeStruct((kept, snaps, lanes), BF16),
            jax.ShapeDtypeStruct((snaps, snaps), F32),
        ],
        scratch_shapes=[
            pltpu.VMEM((steps, comps, cells_y, snaps, cells_z), BF16),
            pltpu.VMEM((kept, comps, 2, snaps, cells_z), BF16),
            pltpu.VMEM((kept, comps, 2, snaps, cells_z), BF16),
            pltpu.VMEM((5, comps, cells_y, snaps, cells_z), F32),
            pltpu.VMEM((3, comps, cells_y, snaps, cells_z), F32),
            pltpu.VMEM((kept, snaps, lanes), BF16),
            DMA((3, steps, 3)),
            DMA((kept,)),
        ],
        compiler_params=PARAMS,
    )(*metrics, *sources, low, high)


def modes_kernel(places, inverse_ref, *rest):
    n = len(rest) - 6
    sources, (out, held, made, rows, in_sems, out_sems) = rest[:n], rest[n:]
    snaps, comps, _, cells_y, cells_z = out.shape

    def reads(x):
        copies, lane = [], 0
        for m, (source, layer, ys) in enumerate(places[x]):
            lanes = pl.ds(lane, comps * len(ys) * cells_z)
            lane += comps * len(ys) * cells_z
            copies.append(
                pltpu.make_async_copy(
                    sources[source].at[layer], held.at[x, :, lanes], in_sems.at[x, m]
                )
            )
        return copies

    for x in range(len(places)):
        for copy in reads(x):
            copy.start()
    writes = []
    for x in range(len(places)):
        for copy in reads(x):
            copy.wait()
        for f in range(comps):
            lane = 0
            for _, _, ys in places[x]:
                width = len(ys) * cells_z
                at = lane + f * width
                lane += comps * width
                whole = jnp.dot(
                    inverse_ref[...], held[x, :, at : at + width], preferred_element_type=F32
                )
                for k, y in enumerate(ys):
                    rows[f % 2, pl.ds(y, snaps, stride=PITCH), :] = whole[
                        :, k * cells_z : (k + 1) * cells_z
                    ]
            for s in range(snaps):
                made[x, s, f] = rows[f % 2, pl.ds(s * PITCH, cells_y), :].astype(BF16)
        writes.append(pltpu.make_async_copy(made.at[x], out.at[:, :, x], out_sems.at[x]))
        writes[-1].start()
    for w in writes:
        w.wait()


def modes(inverse, sources, places, cells_y, cells_z):
    snaps = inverse.shape[0]
    cells_x = len(places)
    return pl.pallas_call(
        functools.partial(modes_kernel, places),
        in_specs=[VMEM] + [HBM] * len(sources),
        out_specs=HBM,
        out_shape=jax.ShapeDtypeStruct((snaps, 4, cells_x, cells_y, cells_z), BF16),
        scratch_shapes=[
            pltpu.VMEM((cells_x, snaps, 4 * cells_y * cells_z), BF16),
            pltpu.VMEM((cells_x, snaps, 4, cells_y, cells_z), BF16),
            pltpu.VMEM((2, snaps * PITCH, cells_z), F32),
            DMA((cells_x, 2)),
            DMA((cells_x,)),
        ],
        compiler_params=PARAMS,
    )(inverse, *sources)


def total(local):
    for axis in ("cross", "stream"):
        count = lax.axis_size(axis)
        if count & (count - 1):
            local = lax.psum(local, axis)
            continue
        step = 1
        while step < count:
            local = local + lax.ppermute(local, axis, [(i, i ^ step) for i in range(count)])
            step *= 2
    return local


def shift(cells, axis, way):
    count = lax.axis_size(axis)
    pairs = [(i, i + way) for i in range(count) if 0 <= i + way < count]
    return lax.ppermute(cells, axis, pairs)


def both_ways(pairs):
    return [p for a, b in pairs for p in ((a, b), (b, a))]


def far_exchange(far2):
    count = lax.axis_size("stream")
    direct = both_ways([(i, i + 1) for i in range(1, count - 1, 2)])
    if count == 4:
        half_way = lax.ppermute(far2, "stream", [(1, 3), (2, 0)])
        return half_way, lambda cells: lax.ppermute(cells, "stream", [(3, 2), (0, 1)]), direct
    return far2, lambda cells: lax.ppermute(cells, "stream", direct), direct


def shards(velocity, metric_x, metric_y, metric_z):
    snaps, comps, cells_x, cells_y, cells_z = velocity.shape
    count = lax.axis_size("stream")
    near, far1, far2, first, last = edges(velocity)
    after_edges, _ = lax.optimization_barrier((velocity, near))
    half_way, second_hop, direct = far_exchange(far2)
    near = lax.ppermute(near, "stream", both_ways([(i, i + 1) for i in range(0, count - 1, 2)]))
    far1 = lax.ppermute(far1, "stream", direct)
    low = shift(last, "cross", 1)
    high = shift(first, "cross", -1)
    cells = planes(after_edges)
    half_way, cells = lax.optimization_barrier((half_way, cells))
    far2 = second_hop(half_way)

    taps = jnp.zeros((cells_z, cells_z), F32)
    for step, weight in ((1, 8.0), (-1, -8.0), (2, -1.0), (-2, 1.0)):
        taps = taps + weight * jnp.eye(cells_z, k=-step, dtype=F32)
    metrics = (metric_x / 12.0, metric_y / 12.0, metric_z[None, :] / 12.0, taps.astype(BF16))
    whole, half = slice(0, cells_y), cells_y // 2

    def local(layer):
        return lambda refs: [(refs[0].at[:, layer], whole, None)]

    def halo(layer, of_near):
        def read(refs):
            odd = lax.rem(lax.axis_index("stream"), 2)
            is_near = (odd == 1) == of_near
            is_far = jnp.logical_not(is_near)
            return [
                (refs[1].at[:, layer], whole, is_near),
                (refs[2].at[:, layer], slice(0, half), is_far),
                (refs[3].at[:, layer], slice(half, cells_y), is_far),
            ]

        return read

    rows = tuple(range(cells_y))
    rows_in, rows_out = rows[2:-2], rows[:2] + rows[-2:]
    walk = ([local(i) for i in range(cells_x)], [None] * 4 + list(range(2, cells_x - 2)))
    middle, middle_gram = fields([cells], *walk, rows_in, first, last, metrics)
    sides, sides_gram = fields([cells], *walk, rows_out, low, high, metrics)
    outer, outer_gram = fields(
        [cells, near, far1, far2],
        [halo(0, True), halo(1, True)]
        + [local(i) for i in (*range(4), *range(cells_x - 4, cells_x))]
        + [halo(0, False), halo(1, False)],
        [None] * 4 + [0, 1] + [None] * 4 + [cells_x - 2, cells_x - 1],
        rows,
        low,
        high,
        metrics,
    )
    everywhere = (
        4.0 * cells_x * lax.axis_size("stream") * cells_y * lax.axis_size("cross") * cells_z
    )
    gram = total(middle_gram + sides_gram + outer_gram)
    lower = jnp.linalg.cholesky(gram * (1.0 / everywhere))
    inverse = jax.scipy.linalg.solve_triangular(lower, jnp.eye(snaps, dtype=F32), lower=True)
    places = [
        [(2, x if x < 2 else x - cells_x + 4, rows)]
        if x < 2 or x >= cells_x - 2
        else [(0, x - 2, rows_in), (1, x - 2, rows_out)]
        for x in range(cells_x)
    ]
    basis = modes(inverse.astype(BF16), [middle, sides, outer], places, cells_y, cells_z)
    return basis, lower


def solution(mesh):
    return jax.shard_map(
        shards,
        mesh=mesh,
        in_specs=(P(None, None, "stream", "cross", None), P("stream"), P("cross"), P()),
        out_specs=(P(None, None, "stream", "cross", None), P()),
        check_vma=False,
    )
```

```python
import functools

import jax
import jax.numpy as jnp
from jax import lax
from jax.experimental import pallas as pl
from jax.experimental.pallas import tpu as pltpu
from jax.sharding import PartitionSpec as P

F32, BF16 = jnp.float32, jnp.bfloat16
VMEM_LIMIT = 56 * 1024 * 1024
PITCH = 9
ROWS = 16
HBM = pl.BlockSpec(memory_space=pl.ANY)
SMEM = pl.BlockSpec(memory_space=pltpu.SMEM)
VMEM = pl.BlockSpec(memory_space=pltpu.VMEM)
PARAMS = pltpu.CompilerParams(vmem_limit_bytes=VMEM_LIMIT)
SHORT = pl.CostEstimate(flops=1024, bytes_accessed=1024, transcendentals=0)
DMA = pltpu.SemaphoreType.DMA


def turn(tile, rows, ys, put):
    snaps, cells_y, cells_z = tile.shape
    wide = tile.astype(F32)
    for s in range(snaps):
        rows[pl.ds(s * PITCH, cells_y), :] = wide[s]
    for y in ys:
        put(y, rows[pl.ds(y, snaps, stride=PITCH), :].astype(BF16))


def edges_kernel(
    velocity, near, far1, far2, first, last, tiles, inner, ends, sides, rows, *sems
):
    end_in, inner_in, end_out, side_out = sems
    snaps, comps, cells_x, cells_y, _ = velocity.shape
    odd = lax.rem(lax.axis_index("stream"), 2)
    firsts = ((1 - odd) * (cells_x - 2), odd * (cells_x - 2))
    half = cells_y // 2
    between = cells_x - 4
    order = [(side, c) for side in (1, 0) for c in range(comps)]

    def end_read(side, c):
        return pltpu.make_async_copy(
            velocity.at[:, c, pl.ds(firsts[side], 2)], tiles.at[side, c], end_in.at[side, c]
        )

    def inner_read(c):
        return pltpu.make_async_copy(
            velocity.at[:, c, pl.ds(2, between)], inner.at[c], inner_in.at[c]
        )

    def side_writes(c, x):
        return [
            pltpu.make_async_copy(sides.at[k, c, x], ref.at[c, x], side_out.at[k, c, x])
            for k, ref in enumerate((first, last))
        ]

    def put_side(c, x, y, plane):
        if y < 2:
            sides[0, c, x, y] = plane
        elif y >= cells_y - 2:
            sides[1, c, x, y - cells_y + 2] = plane

    for side, c in order:
        end_read(side, c).start()
    for c in range(comps):
        inner_read(c).start()
    writes = []
    for side, c in order:
        end_read(side, c).wait()

        def one_end(layer, _):
            x = firsts[side] + layer

            def put(y, plane):
                ends[side, c, layer, y] = plane
                put_side(c, x, y, plane)

            turn(tiles[side, c, :, layer], rows, range(cells_y), put)
            for w in side_writes(c, x):
                w.start()
            return 0

        lax.fori_loop(0, 2, one_end, 0)
        if side == 0:
            parts = [(ends.at[0, c], near.at[c])]
        else:
            parts = [
                (ends.at[1, c, :, pl.ds(0, half)], far1.at[c]),
                (ends.at[1, c, :, pl.ds(half, half)], far2.at[c]),
            ]
        for src, dst in parts:
            writes.append(pltpu.make_async_copy(src, dst, end_out.at[len(writes)]))
            writes[-1].start()

    for c in range(comps):
        inner_read(c).wait()

        def one_inner(n, _):
            turn(
                inner[c, :, n],
                rows,
                (0, 1, cells_y - 2, cells_y - 1),
                functools.partial(put_side, c, n + 2),
            )
            for w in side_writes(c, n + 2):
                w.start()
            return 0

        lax.fori_loop(0, between, one_inner, 0)

    for w in writes:
        w.wait()

    def finish(n, _):
        for w in side_writes(n // cells_x, lax.rem(n, cells_x)):
            w.wait()
        return 0

    lax.fori_loop(0, comps * cells_x, finish, 0)


def edges(velocity):
    snaps, comps, cells_x, cells_y, cells_z = velocity.shape
    shape = lambda layers, rows: jax.ShapeDtypeStruct((comps, layers, rows, snaps, cells_z), BF16)
    return pl.pallas_call(
        edges_kernel,
        in_specs=[HBM],
        out_specs=[HBM] * 5,
        out_shape=[shape(2, cells_y)] + [shape(2, cells_y // 2)] * 2 + [shape(cells_x, 2)] * 2,
        scratch_shapes=[
            pltpu.VMEM((2, comps, snaps, 2, cells_y, cells_z), BF16),
            pltpu.VMEM((comps, snaps, cells_x - 4, cells_y, cells_z), BF16),
            pltpu.VMEM((2, comps, 2, cells_y, snaps, cells_z), BF16),
            pltpu.VMEM((2, comps, cells_x, 2, snaps, cells_z), BF16),
            pltpu.VMEM((snaps * PITCH, cells_z), F32),
            DMA((2, comps)),
            DMA((comps,)),
            DMA((3 * comps,)),
            DMA((2, comps, cells_x)),
        ],
        compiler_params=PARAMS,
    )(velocity)


def planes_kernel(velocity, cells, taken, turned, rows, in_sems, out_sems):
    snaps, comps, cells_x, cells_y, cells_z = velocity.shape

    def read(c, x):
        return pltpu.make_async_copy(velocity.at[:, c, x], taken.at[c, x], in_sems.at[c, x])

    def write(c, x):
        return pltpu.make_async_copy(turned.at[c, x], cells.at[c, x], out_sems.at[c, x])

    def each(work):
        def step(n, _):
            work(n // cells_x, lax.rem(n, cells_x))
            return 0

        lax.fori_loop(0, comps * cells_x, step, 0)

    def one(c, x):
        read(c, x).wait()

        def put(y, plane):
            turned[c, x, y] = plane

        turn(taken[c, x], rows, range(cells_y), put)
        write(c, x).start()

    each(lambda c, x: read(c, x).start())
    each(one)
    each(lambda c, x: write(c, x).wait())


def planes(velocity):
    snaps, comps, cells_x, cells_y, cells_z = velocity.shape
    return pl.pallas_call(
        planes_kernel,
        in_specs=[HBM],
        out_specs=HBM,
        out_shape=jax.ShapeDtypeStruct((comps, cells_x, cells_y, snaps, cells_z), BF16),
        scratch_shapes=[
            pltpu.VMEM((comps, cells_x, snaps, cells_y, cells_z), BF16),
            pltpu.VMEM((comps, cells_x, cells_y, snaps, cells_z), BF16),
            pltpu.VMEM((snaps * PITCH, cells_z), F32),
            DMA((comps, cells_x)),
            DMA((comps, cells_x)),
        ],
        compiler_params=PARAMS,
    )(velocity)


def layer_fields(ys, ring, slots, rz, low, high, metric_x, metric_y_ref, metric_z, out_ref):
    cells_y, snaps, cells_z = ring.shape[2:]
    back2, back1, here, fore1, fore2 = slots

    def some_rows(step, _):
        at = pl.ds(pl.multiple_of(step * ROWS, ROWS), ROWS)
        held = {}

        def row(comp, y):
            if (comp, y) not in held:
                if y < 0:
                    held[comp, y] = low[comp, y + 2, at, :].astype(F32)
                elif y >= cells_y:
                    held[comp, y] = high[comp, y - cells_y, at, :].astype(F32)
                else:
                    held[comp, y] = ring[here, comp, y, at, :]
            return held[comp, y]

        for n, y in enumerate(ys):

            def along_x(c):
                near = ring[fore1, c, y, at, :] - ring[back1, c, y, at, :]
                far = ring[fore2, c, y, at, :] - ring[back2, c, y, at, :]
                return (8.0 * near - far) * metric_x

            def along_y(c):
                near = row(c, y + 1) - row(c, y - 1)
                far = row(c, y + 2) - row(c, y - 2)
                return (8.0 * near - far) * metric_y_ref[y]

            def along_z(c):
                return rz[c, y, at, :] * metric_z

            outs = (
                along_y(2) - along_z(1),
                along_z(0) - along_x(2),
                along_x(1) - along_y(0),
                along_x(0) + along_y(1) + along_z(2),
            )
            for f, value in enumerate(outs):
                lane = (f * len(ys) + n) * cells_z
                out_ref[at, lane : lane + cells_z] = value.astype(BF16)
        return 0

    lax.fori_loop(0, snaps // ROWS, some_rows, 0)


def runs(ys):
    found = []
    for y in ys:
        if found and found[-1][1] == y:
            found[-1][1] = y + 1
        else:
            found.append([y, y + 1])
    return found


def fields_kernel(reads, centers, ys, mx_ref, my_ref, mz_ref, taps_ref, *rest):
    n = len(rest) - 12
    sources, (low, high, out, gram_ref) = rest[:n], rest[n : n + 4]
    layers, lows, highs, ring, rz_ring, done, in_sems, out_sems = rest[n + 4 :]
    comps, cells_y, snaps, cells_z = ring.shape[1:]
    steps = len(centers)
    kept = [i for i in range(steps) if centers[i] is not None]
    lowest, highest = min(ys) < 2, max(ys) >= cells_y - 2

    def whichever(i, start):
        for m, (src, rows, cond) in enumerate(reads[i](sources)):
            copy = pltpu.make_async_copy(src, layers.at[i, :, rows], in_sems.at[0, i, m])
            if cond is None:
                getattr(copy, "start" if start else "wait")()
            else:
                pl.when(cond)(copy.start if start else copy.wait)

    def sides(k):
        x = centers[kept[k]]
        copies = []
        if lowest:
            copies.append(pltpu.make_async_copy(low.at[:, x], lows.at[k], in_sems.at[1, k, 0]))
        if highest:
            copies.append(pltpu.make_async_copy(high.at[:, x], highs.at[k], in_sems.at[2, k, 0]))
        return copies

    for i in range(steps):
        whichever(i, True)
        if centers[i] is not None:
            for copy in sides(kept.index(i)):
                copy.start()

    gram_ref[...] = jnp.zeros_like(gram_ref)
    writes = []
    for i in range(steps):
        whichever(i, False)
        ring[i % 5] = layers[i].astype(F32)
        if i + 2 < steps and centers[i + 2] is not None:
            for a, b in runs(ys):
                flat = layers[i, :, a:b].reshape(comps * (b - a) * snaps, cells_z)
                rz_ring[i % 3, :, a:b] = jnp.dot(
                    flat, taps_ref[...], preferred_element_type=F32
                ).reshape(comps, b - a, snaps, cells_z)
        if centers[i] is None:
            continue
        k = kept.index(i)
        for copy in sides(k):
            copy.wait()
        layer_fields(
            ys,
            ring,
            [(i + 1 + s) % 5 for s in range(5)],
            rz_ring.at[(i - 2) % 3],
            lows.at[k],
            highs.at[k],
            mx_ref[centers[i]],
            my_ref,
            mz_ref[...],
            done.at[k],
        )
        writes.append(pltpu.make_async_copy(done.at[k], out.at[k], out_sems.at[k]))
        writes[-1].start()
        gram_ref[...] += lax.dot_general(
            done[k], done[k], (((1,), (1,)), ((), ())), preferred_element_type=F32
        )
    for w in writes:
        w.wait()


def fields(sources, reads, centers, ys, low, high, metrics):
    comps, _, cells_y, snaps, cells_z = sources[0].shape
    steps = len(centers)
    kept = sum(c is not None for c in centers)
    lanes = 4 * len(ys) * cells_z
    return pl.pallas_call(
        functools.partial(fields_kernel, reads, centers, ys),
        in_specs=[SMEM, SMEM, VMEM, VMEM] + [HBM] * (len(sources) + 2),
        out_specs=[HBM, VMEM],
        out_shape=[
            jax.ShapeDtypeStruct((kept, snaps, lanes), BF16),
            jax.ShapeDtypeStruct((snaps, snaps), F32),
        ],
        scratch_shapes=[
            pltpu.VMEM((steps, comps, cells_y, snaps, cells_z), BF16),
            pltpu.VMEM((kept, comps, 2, snaps, cells_z), BF16),
            pltpu.VMEM((kept, comps, 2, snaps, cells_z), BF16),
            pltpu.VMEM((5, comps, cells_y, snaps, cells_z), F32),
            pltpu.VMEM((3, comps, cells_y, snaps, cells_z), F32),
            pltpu.VMEM((kept, snaps, lanes), BF16),
            DMA((3, steps, 3)),
            DMA((kept,)),
        ],
        compiler_params=PARAMS,
    )(*metrics, *sources, low, high)


def factorize(rows, panel):
    eight, n = rows[0].shape
    shape = (eight, n)
    sub = lax.broadcasted_iota(jnp.int32, shape, 0)
    lane = lax.broadcasted_iota(jnp.int32, shape, 1)
    rows = list(rows)
    eyes = [jnp.where(lane == sub + eight * j, 1.0, 0.0).astype(F32) for j in range(len(rows))]
    uppers, inverses = [], []

    def spread(block, r):
        return jnp.broadcast_to(block[r : r + 1], shape)

    def join(parts):
        out = parts[0]
        for r in range(1, eight):
            out = jnp.where(sub == r, parts[r], out)
        return out

    for first in range(0, len(rows), panel):
        rest = first + panel
        for j in range(first, rest):
            at = eight * j
            left = {
                (r, c): jnp.broadcast_to(rows[j][r : r + 1, at + c : at + c + 1], shape)
                for r in range(eight)
                for c in range(r + 1)
            }
            upper = [spread(rows[j], r) for r in range(eight)]
            inverse = [spread(eyes[j], r) for r in range(eight)]
            for c in range(eight):
                root = lax.rsqrt(left[c, c])
                column = {r: left[r, c] * root for r in range(c + 1, eight)}
                for k in range(c + 1, eight):
                    for r in range(k, eight):
                        left[r, k] = left[r, k] - column[r] * column[k]
                upper[c] = upper[c] * root
                inverse[c] = inverse[c] * root
                for r in range(c + 1, eight):
                    upper[r] = upper[r] - column[r] * upper[c]
                    inverse[r] = inverse[r] - column[r] * inverse[c]
            for k in range(j + 1, rest):
                own = lane == sub + eight * k
                turned = [
                    jnp.sum(jnp.where(own, u, 0.0), axis=1, keepdims=True) for u in upper
                ]
                rows[k] = rows[k] - sum(t * u for t, u in zip(turned, upper))
                eyes[k] = eyes[k] - sum(t * v for t, v in zip(turned, inverse))
            uppers.append(join(upper))
            inverses.append(join(inverse))
        if rest < len(rows):
            u = jnp.concatenate(uppers[first:rest], axis=0)
            v = jnp.concatenate(inverses[first:rest], axis=0)
            below = u.T[eight * rest :]
            dot = functools.partial(
                jnp.dot, precision=lax.Precision.HIGHEST, preferred_element_type=F32
            )
            du, dv = dot(below, u), dot(below, v)
            for k in range(rest, len(rows)):
                o = slice(eight * (k - rest), eight * (k - rest + 1))
                rows[k] = rows[k] - du[o]
                eyes[k] = eyes[k] - dv[o]
    return jnp.concatenate(uppers, axis=0), jnp.concatenate(inverses, axis=0)


def modes_kernel(places, scale, gram_ref, more_ref, *rest):
    n = len(rest) - 7
    sources, (out, lower_ref, held, made, rows, in_sems, out_sems) = rest[:n], rest[n:]
    snaps, comps, _, cells_y, cells_z = out.shape

    def reads(x):
        copies, lane = [], 0
        for m, (source, layer, ys) in enumerate(places[x]):
            lanes = pl.ds(lane, comps * len(ys) * cells_z)
            lane += comps * len(ys) * cells_z
            copies.append(
                pltpu.make_async_copy(
                    sources[source].at[layer], held.at[x, :, lanes], in_sems.at[x, m]
                )
            )
        return copies

    for x in range(len(places)):
        for copy in reads(x):
            copy.start()

    upper, inverse = factorize(
        [
            (gram_ref[r : r + 8, :] + more_ref[r : r + 8, :]) * scale
            for r in range(0, snaps, 8)
        ],
        4,
    )
    r = lax.broadcasted_iota(jnp.int32, (snaps, snaps), 0)
    c = lax.broadcasted_iota(jnp.int32, (snaps, snaps), 1)
    lower_ref[...] = jnp.where(r >= c, upper.T, 0.0)
    inverse = inverse.astype(BF16)

    writes = []
    for x in range(len(places)):
        for copy in reads(x):
            copy.wait()
        for f in range(comps):
            lane = 0
            for _, _, ys in places[x]:
                width = len(ys) * cells_z
                at = lane + f * width
                lane += comps * width
                whole = jnp.dot(inverse, held[x, :, at : at + width], preferred_element_type=F32)
                for k, y in enumerate(ys):
                    rows[f % 2, pl.ds(y, snaps, stride=PITCH), :] = whole[
                        :, k * cells_z : (k + 1) * cells_z
                    ]
            for s in range(snaps):
                made[x, s, f] = rows[f % 2, pl.ds(s * PITCH, cells_y), :].astype(BF16)
        writes.append(pltpu.make_async_copy(made.at[x], out.at[:, :, x], out_sems.at[x]))
        writes[-1].start()
    for w in writes:
        w.wait()


def modes(gram, more, scale, sources, places, cells_y, cells_z):
    snaps = gram.shape[0]
    cells_x = len(places)
    return pl.pallas_call(
        functools.partial(modes_kernel, places, scale),
        in_specs=[VMEM, VMEM] + [HBM] * len(sources),
        out_specs=[HBM, VMEM],
        out_shape=[
            jax.ShapeDtypeStruct((snaps, 4, cells_x, cells_y, cells_z), BF16),
            jax.ShapeDtypeStruct((snaps, snaps), F32),
        ],
        scratch_shapes=[
            pltpu.VMEM((cells_x, snaps, 4 * cells_y * cells_z), BF16),
            pltpu.VMEM((cells_x, snaps, 4, cells_y, cells_z), BF16),
            pltpu.VMEM((2, snaps * PITCH, cells_z), F32),
            DMA((cells_x, 2)),
            DMA((cells_x,)),
        ],
        compiler_params=PARAMS,
    )(gram, more, *sources)


def total(local):
    steps = []
    for axis in ("cross", "stream"):
        count = lax.axis_size(axis)
        steps += [(axis, count, 1 << k) for k in range((count - 1).bit_length())]
    more = jnp.zeros_like(local)
    for axis, count, step in steps:
        local = local + more
        more = lax.ppermute(local, axis, [(i, i ^ step) for i in range(count)])
    return local, more


def shift(cells, axis, way):
    count = lax.axis_size(axis)
    pairs = [(i, i + way) for i in range(count) if 0 <= i + way < count]
    return lax.ppermute(cells, axis, pairs)


def both_ways(pairs):
    return [p for a, b in pairs for p in ((a, b), (b, a))]


def far_exchange(far2):
    count = lax.axis_size("stream")
    direct = both_ways([(i, i + 1) for i in range(1, count - 1, 2)])
    if count == 4:
        half_way = lax.ppermute(far2, "stream", [(1, 3), (2, 0)])
        return half_way, lambda cells: lax.ppermute(cells, "stream", [(3, 2), (0, 1)]), direct
    return far2, lambda cells: lax.ppermute(cells, "stream", direct), direct


def shards(velocity, metric_x, metric_y, metric_z):
    snaps, comps, cells_x, cells_y, cells_z = velocity.shape
    count = lax.axis_size("stream")
    near, far1, far2, first, last = edges(velocity)
    after_edges, _ = lax.optimization_barrier((velocity, near))
    half_way, second_hop, direct = far_exchange(far2)
    near = lax.ppermute(near, "stream", both_ways([(i, i + 1) for i in range(0, count - 1, 2)]))
    far1 = lax.ppermute(far1, "stream", direct)
    low = shift(last, "cross", 1)
    high = shift(first, "cross", -1)
    cells = planes(after_edges)
    half_way, cells = lax.optimization_barrier((half_way, cells))
    far2 = second_hop(half_way)

    taps = jnp.zeros((cells_z, cells_z), F32)
    for step, weight in ((1, 8.0), (-1, -8.0), (2, -1.0), (-2, 1.0)):
        taps = taps + weight * jnp.eye(cells_z, k=-step, dtype=F32)
    metrics = (metric_x / 12.0, metric_y / 12.0, metric_z[None, :] / 12.0, taps.astype(BF16))
    whole, half = slice(0, cells_y), cells_y // 2

    def local(layer):
        return lambda refs: [(refs[0].at[:, layer], whole, None)]

    def halo(layer, of_near):
        def read(refs):
            odd = lax.rem(lax.axis_index("stream"), 2)
            is_near = (odd == 1) == of_near
            is_far = jnp.logical_not(is_near)
            return [
                (refs[1].at[:, layer], whole, is_near),
                (refs[2].at[:, layer], slice(0, half), is_far),
                (refs[3].at[:, layer], slice(half, cells_y), is_far),
            ]

        return read

    rows = tuple(range(cells_y))
    rows_in, rows_out = rows[2:-2], rows[:2] + rows[-2:]
    walk = ([local(i) for i in range(cells_x)], [None] * 4 + list(range(2, cells_x - 2)))
    middle, middle_gram = fields([cells], *walk, rows_in, first, last, metrics)
    sides, sides_gram = fields([cells], *walk, rows_out, low, high, metrics)
    outer, outer_gram = fields(
        [cells, near, far1, far2],
        [halo(0, True), halo(1, True)]
        + [local(i) for i in (*range(4), *range(cells_x - 4, cells_x))]
        + [halo(0, False), halo(1, False)],
        [None] * 4 + [0, 1] + [None] * 4 + [cells_x - 2, cells_x - 1],
        rows,
        low,
        high,
        metrics,
    )
    everywhere = (
        4.0 * cells_x * lax.axis_size("stream") * cells_y * lax.axis_size("cross") * cells_z
    )
    gram, more = total(middle_gram + sides_gram + outer_gram)
    places = [
        [(2, x if x < 2 else x - cells_x + 4, rows)]
        if x < 2 or x >= cells_x - 2
        else [(0, x - 2, rows_in), (1, x - 2, rows_out)]
        for x in range(cells_x)
    ]
    sources = [middle, sides, outer]
    return tuple(modes(gram, more, 1.0 / everywhere, sources, places, cells_y, cells_z))


def solution(mesh):
    return jax.shard_map(
        shards,
        mesh=mesh,
        in_specs=(P(None, None, "stream", "cross", None), P("stream"), P("cross"), P()),
        out_specs=(P(None, None, "stream", "cross", None), P()),
        check_vma=False,
    )
```

```python
import functools

import jax
import jax.numpy as jnp
from jax import lax
from jax.experimental import pallas as pl
from jax.experimental.pallas import tpu as pltpu
from jax.sharding import PartitionSpec as P

F32, BF16 = jnp.float32, jnp.bfloat16
PITCH = 9
ROWS = 16
SLOTS = 4
HBM = pl.BlockSpec(memory_space=pl.ANY)
SMEM = pl.BlockSpec(memory_space=pltpu.SMEM)
VMEM = pl.BlockSpec(memory_space=pltpu.VMEM)
DMA = pltpu.SemaphoreType.DMA


def limit(mib):
    return pltpu.CompilerParams(vmem_limit_bytes=mib * 1024 * 1024)


def turn(tile, rows, ys, put):
    snaps, cells_y, cells_z = tile.shape
    wide = tile.astype(F32)
    for s in range(snaps):
        rows[pl.ds(s * PITCH, cells_y), :] = wide[s]
    for y in ys:
        put(y, rows[pl.ds(y, snaps, stride=PITCH), :].astype(BF16))


def edges_kernel(
    velocity, near, far1, far2, first, last, tiles, inner, ends, sides, rows, *sems
):
    end_in, inner_in, end_out, side_out = sems
    snaps, comps, cells_x, cells_y, _ = velocity.shape
    odd = lax.rem(lax.axis_index("stream"), 2)
    firsts = ((1 - odd) * (cells_x - 2), odd * (cells_x - 2))
    half = cells_y // 2
    between = cells_x - 4
    order = [(side, c) for side in (1, 0) for c in range(comps)]

    def end_read(side, c):
        return pltpu.make_async_copy(
            velocity.at[:, c, pl.ds(firsts[side], 2)], tiles.at[side, c], end_in.at[side, c]
        )

    def inner_read(c):
        return pltpu.make_async_copy(
            velocity.at[:, c, pl.ds(2, between)], inner.at[c], inner_in.at[c]
        )

    def side_writes(c, x):
        return [
            pltpu.make_async_copy(sides.at[k, c, x], ref.at[c, x], side_out.at[k, c, x])
            for k, ref in enumerate((first, last))
        ]

    def put_side(c, x, y, plane):
        if y < 2:
            sides[0, c, x, y] = plane
        elif y >= cells_y - 2:
            sides[1, c, x, y - cells_y + 2] = plane

    for side, c in order:
        end_read(side, c).start()
    for c in range(comps):
        inner_read(c).start()
    writes = []
    for side, c in order:
        end_read(side, c).wait()

        def one_end(layer, _):
            x = firsts[side] + layer

            def put(y, plane):
                ends[side, c, layer, y] = plane
                put_side(c, x, y, plane)

            turn(tiles[side, c, :, layer], rows, range(cells_y), put)
            for w in side_writes(c, x):
                w.start()
            return 0

        lax.fori_loop(0, 2, one_end, 0)
        if side == 0:
            parts = [(ends.at[0, c], near.at[c])]
        else:
            parts = [
                (ends.at[1, c, :, pl.ds(0, half)], far1.at[c]),
                (ends.at[1, c, :, pl.ds(half, half)], far2.at[c]),
            ]
        for src, dst in parts:
            writes.append(pltpu.make_async_copy(src, dst, end_out.at[len(writes)]))
            writes[-1].start()

    for c in range(comps):
        inner_read(c).wait()

        def one_inner(n, _):
            turn(
                inner[c, :, n],
                rows,
                (0, 1, cells_y - 2, cells_y - 1),
                functools.partial(put_side, c, n + 2),
            )
            for w in side_writes(c, n + 2):
                w.start()
            return 0

        lax.fori_loop(0, between, one_inner, 0)

    for w in writes:
        w.wait()

    def finish(n, _):
        for w in side_writes(n // cells_x, lax.rem(n, cells_x)):
            w.wait()
        return 0

    lax.fori_loop(0, comps * cells_x, finish, 0)


def edges(velocity):
    snaps, comps, cells_x, cells_y, cells_z = velocity.shape
    shape = lambda layers, rows: jax.ShapeDtypeStruct((comps, layers, rows, snaps, cells_z), BF16)
    return pl.pallas_call(
        edges_kernel,
        in_specs=[HBM],
        out_specs=[HBM] * 5,
        out_shape=[shape(2, cells_y)] + [shape(2, cells_y // 2)] * 2 + [shape(cells_x, 2)] * 2,
        scratch_shapes=[
            pltpu.VMEM((2, comps, snaps, 2, cells_y, cells_z), BF16),
            pltpu.VMEM((comps, snaps, cells_x - 4, cells_y, cells_z), BF16),
            pltpu.VMEM((2, comps, 2, cells_y, snaps, cells_z), BF16),
            pltpu.VMEM((2, comps, cells_x, 2, snaps, cells_z), BF16),
            pltpu.VMEM((snaps * PITCH, cells_z), F32),
            DMA((2, comps)),
            DMA((comps,)),
            DMA((3 * comps,)),
            DMA((2, comps, cells_x)),
        ],
        compiler_params=limit(60),
    )(velocity)


def planes_kernel(velocity, cells, taken, turned, rows, in_sems, out_sems):
    snaps, comps, cells_x, cells_y, cells_z = velocity.shape

    def read(c, x):
        return pltpu.make_async_copy(velocity.at[:, c, x], taken.at[c, x], in_sems.at[c, x])

    def write(c, x):
        return pltpu.make_async_copy(turned.at[c, x], cells.at[c, x], out_sems.at[c, x])

    def each(work):
        def step(n, _):
            work(n // cells_x, lax.rem(n, cells_x))
            return 0

        lax.fori_loop(0, comps * cells_x, step, 0)

    def one(c, x):
        read(c, x).wait()

        def put(y, plane):
            turned[c, x, y] = plane

        turn(taken[c, x], rows, range(cells_y), put)
        write(c, x).start()

    each(lambda c, x: read(c, x).start())
    each(one)
    each(lambda c, x: write(c, x).wait())


def planes(velocity):
    snaps, comps, cells_x, cells_y, cells_z = velocity.shape
    return pl.pallas_call(
        planes_kernel,
        in_specs=[HBM],
        out_specs=HBM,
        out_shape=jax.ShapeDtypeStruct((comps, cells_x, cells_y, snaps, cells_z), BF16),
        scratch_shapes=[
            pltpu.VMEM((comps, cells_x, snaps, cells_y, cells_z), BF16),
            pltpu.VMEM((comps, cells_x, cells_y, snaps, cells_z), BF16),
            pltpu.VMEM((snaps * PITCH, cells_z), F32),
            DMA((comps, cells_x)),
            DMA((comps, cells_x)),
        ],
        compiler_params=limit(60),
    )(velocity)


def layer_fields(ring, slots, rz, low, high, metric_x, metric_y_ref, metric_z, puts):
    cells_y, snaps, cells_z = ring.shape[2:]
    back2, back1, here, fore1, fore2 = slots

    def some_rows(step, _):
        at = pl.ds(pl.multiple_of(step * ROWS, ROWS), ROWS)

        def row(comp, y):
            if y < 0:
                return low[comp, y + 2, at, :].astype(F32)
            if y >= cells_y:
                return high[comp, y - cells_y, at, :].astype(F32)
            return ring[here, comp, y, at, :]

        window = [[row(c, y) for y in range(-2, 2)] for c in range(3)]
        for y in range(cells_y):
            for c in range(3):
                window[c].append(row(c, y + 2))

            def along_x(c):
                near = ring[fore1, c, y, at, :] - ring[back1, c, y, at, :]
                far = ring[fore2, c, y, at, :] - ring[back2, c, y, at, :]
                return (8.0 * near - far) * metric_x

            def along_y(c):
                w = window[c]
                return (8.0 * (w[3] - w[1]) - (w[4] - w[0])) * metric_y_ref[y]

            def along_z(c):
                return rz[c, y, at, :] * metric_z

            puts[0](at, y, along_y(2) - along_z(1))
            puts[1](at, y, along_z(0) - along_x(2))
            puts[2](at, y, along_x(1) - along_y(0))
            puts[3](at, y, along_x(0) + along_y(1) + along_z(2))
            for c in range(3):
                window[c] = window[c][1:]
        return 0

    lax.fori_loop(0, snaps // ROWS, some_rows, 0)


def inner_kernel(mx_ref, my_ref, mz_ref, taps_ref, cells, low, high, *rest):
    middle, ends, parts, gram_ref = rest[:4]
    layers, lows, highs, ring, rz_ring, done, done_ends, done_parts, in_sems, out_sems = rest[4:]
    comps, cells_y, snaps, cells_z = ring.shape[1:]
    cells_x = lows.shape[0]
    width = cells_y * cells_z

    def reads(x):
        return [
            pltpu.make_async_copy(cells.at[:, x], layers.at[x % SLOTS], in_sems.at[0, x]),
            pltpu.make_async_copy(low.at[:, x], lows.at[x], in_sems.at[1, x]),
            pltpu.make_async_copy(high.at[:, x], highs.at[x], in_sems.at[2, x]),
        ]

    def put_in(ref, lane):
        def put(at, y, value):
            ref[at, lane + y * cells_z : lane + (y + 1) * cells_z] = value.astype(ref.dtype)

        return put

    for x in range(SLOTS):
        for copy in reads(x):
            copy.start()
    gram_ref[...] = jnp.zeros_like(gram_ref)
    writes, middle_writes = [], []

    def write(src, dst):
        sem = out_sems.at[len(writes) + len(middle_writes)]
        writes.append(pltpu.make_async_copy(src, dst, sem))
        writes[-1].start()

    for i in range(cells_x + 4):
        if 2 <= i < cells_x + 2:
            for copy in reads(i - 2):
                copy.wait()
            slot = layers.at[(i - 2) % SLOTS]
            ring[i % 5] = slot[...].astype(F32)
            flat = slot[...].reshape(comps * cells_y * snaps, cells_z)
            rz_ring[i % 3] = jnp.dot(flat, taps_ref[...], preferred_element_type=F32).reshape(
                comps, cells_y, snaps, cells_z
            )
            if i - 2 + SLOTS < cells_x:
                for copy in reads(i - 2 + SLOTS):
                    copy.start()
        else:
            ring[i % 5] = jnp.zeros(ring.shape[1:], F32)
        x = i - 4
        if x < 0:
            continue
        is_inner = 2 <= x < cells_x - 2
        e = x if x < 2 else x - cells_x + 4
        if is_inner:
            made = done.at[x % SLOTS]
            if x - 2 >= SLOTS:
                middle_writes[x - 2 - SLOTS].wait()
            puts = [put_in(made, f * width) for f in range(4)]
        else:
            made = done_ends.at[e]
            puts = [put_in(made, 0)]
            puts += [put_in(done_parts.at[e], f * width) for f in range(3)]
        layer_fields(
            ring,
            [(i + 1 + s) % 5 for s in range(5)],
            rz_ring.at[(i - 2) % 3],
            lows.at[x],
            highs.at[x],
            mx_ref[x],
            my_ref,
            mz_ref[...],
            puts,
        )
        if is_inner:
            write(made, middle.at[x - 2])
            middle_writes.append(writes.pop())
        else:
            write(made, ends.at[e])
            write(done_parts.at[e], parts.at[e])
        gram_ref[...] += lax.dot_general(
            made[...], made[...], (((1,), (1,)), ((), ())), preferred_element_type=F32
        )
    for w in writes + middle_writes[-SLOTS:]:
        w.wait()


def inner_fields(cells, low, high, metrics):
    comps, cells_x, cells_y, snaps, cells_z = cells.shape
    width = cells_y * cells_z
    return pl.pallas_call(
        inner_kernel,
        in_specs=[SMEM, SMEM, VMEM, VMEM] + [HBM] * 3,
        out_specs=[HBM] * 3 + [VMEM],
        out_shape=[
            jax.ShapeDtypeStruct((cells_x - 4, snaps, 4 * width), BF16),
            jax.ShapeDtypeStruct((4, snaps, width), BF16),
            jax.ShapeDtypeStruct((4, snaps, 3 * width), F32),
            jax.ShapeDtypeStruct((snaps, snaps), F32),
        ],
        scratch_shapes=[
            pltpu.VMEM((SLOTS, comps, cells_y, snaps, cells_z), BF16),
            pltpu.VMEM((cells_x, comps, 2, snaps, cells_z), BF16),
            pltpu.VMEM((cells_x, comps, 2, snaps, cells_z), BF16),
            pltpu.VMEM((5, comps, cells_y, snaps, cells_z), F32),
            pltpu.VMEM((3, comps, cells_y, snaps, cells_z), F32),
            pltpu.VMEM((SLOTS, snaps, 4 * width), BF16),
            pltpu.VMEM((4, snaps, width), BF16),
            pltpu.VMEM((4, snaps, 3 * width), F32),
            DMA((3, cells_x)),
            DMA((cells_x + 4,)),
        ],
        compiler_params=limit(36),
    )(*metrics, cells, low, high)


def outer_kernel(near, far1, far2, parts, mx_ref, gram_ref, out, total_ref, *rest):
    taken, halos, done, part_sems, halo_sems, out_sems = rest
    _, comps, _, cells_y, snaps, cells_z = halos.shape
    half = cells_y // 2
    width = cells_y * cells_z
    cells_x = mx_ref.shape[0]
    odd = lax.rem(lax.axis_index("stream"), 2)

    def part_read(e):
        return pltpu.make_async_copy(parts.at[e], taken.at[e], part_sems.at[e])

    def halo_reads(side, run):
        sem = halo_sems.at[side]
        is_near = (odd == 1) == (side == 0)
        first, second = pl.ds(0, half), pl.ds(half, half)

        @pl.when(is_near)
        def _():
            run(pltpu.make_async_copy(near, halos.at[side], sem.at[0]))

        @pl.when(jnp.logical_not(is_near))
        def _():
            run(pltpu.make_async_copy(far1, halos.at[side, :, :, first], sem.at[0]))
            run(pltpu.make_async_copy(far2, halos.at[side, :, :, second], sem.at[1]))

    for side in range(2):
        halo_reads(side, lambda copy: copy.start())
        for e in (2 * side, 2 * side + 1):
            part_read(e).start()
    total = gram_ref[...]
    writes = []
    last = cells_x - 1
    plan = (
        (0, 0, 0, (1.0, -8.0)),
        (1, 1, 0, (0.0, 1.0)),
        (2, last - 1, 1, (-1.0, 0.0)),
        (3, last, 1, (8.0, -1.0)),
    )
    for e, x, side, weights in plan:
        if e % 2 == 0:
            halo_reads(side, lambda copy: copy.wait())
        part_read(e).wait()
        metric_x = mx_ref[x]

        def some_rows(step, _):
            at = pl.ds(pl.multiple_of(step * ROWS, ROWS), ROWS)
            for f, (comp, sign) in enumerate(((2, -1.0), (1, 1.0), (0, 1.0))):
                for y in range(cells_y):
                    lanes = slice(f * width + y * cells_z, f * width + (y + 1) * cells_z)
                    sums = [
                        (sign * w) * halos[side, comp, k, y, at, :].astype(F32)
                        for k, w in enumerate(weights)
                        if w
                    ]
                    value = taken[e, at, lanes] + functools.reduce(jnp.add, sums) * metric_x
                    done[e, at, lanes] = value.astype(BF16)
            return 0

        lax.fori_loop(0, snaps // ROWS, some_rows, 0)
        writes.append(pltpu.make_async_copy(done.at[e], out.at[e], out_sems.at[e]))
        writes[-1].start()
        total += lax.dot_general(
            done[e], done[e], (((1,), (1,)), ((), ())), preferred_element_type=F32
        )
    total_ref[...] = total
    for w in writes:
        w.wait()


def outer_fields(metric_x, gram, parts, near, far1, far2):
    comps, _, cells_y, snaps, cells_z = near.shape
    lanes = parts.shape[2]
    return pl.pallas_call(
        outer_kernel,
        in_specs=[HBM] * 4 + [SMEM, VMEM],
        out_specs=[HBM, VMEM],
        out_shape=[
            jax.ShapeDtypeStruct(parts.shape, BF16),
            jax.ShapeDtypeStruct((snaps, snaps), F32),
        ],
        scratch_shapes=[
            pltpu.VMEM(parts.shape, F32),
            pltpu.VMEM((2, comps, 2, cells_y, snaps, cells_z), BF16),
            pltpu.VMEM(parts.shape, BF16),
            DMA((4,)),
            DMA((2, 2)),
            DMA((4,)),
        ],
        compiler_params=limit(20),
    )(near, far1, far2, parts, metric_x, gram)


def factorize(rows, panel):
    eight, n = rows[0].shape
    shape = (eight, n)
    sub = lax.broadcasted_iota(jnp.int32, shape, 0)
    lane = lax.broadcasted_iota(jnp.int32, shape, 1)
    rows = list(rows)
    eyes = [jnp.where(lane == sub + eight * j, 1.0, 0.0).astype(F32) for j in range(len(rows))]
    uppers, inverses = [], []

    def spread(block, r):
        return jnp.broadcast_to(block[r : r + 1], shape)

    def join(parts):
        out = parts[0]
        for r in range(1, eight):
            out = jnp.where(sub == r, parts[r], out)
        return out

    for first in range(0, len(rows), panel):
        rest = first + panel
        for j in range(first, rest):
            at = eight * j
            left = {
                (r, c): jnp.broadcast_to(rows[j][r : r + 1, at + c : at + c + 1], shape)
                for r in range(eight)
                for c in range(r + 1)
            }
            upper = [spread(rows[j], r) for r in range(eight)]
            inverse = [spread(eyes[j], r) for r in range(eight)]
            for c in range(eight):
                root = lax.rsqrt(left[c, c])
                column = {r: left[r, c] * root for r in range(c + 1, eight)}
                for k in range(c + 1, eight):
                    for r in range(k, eight):
                        left[r, k] = left[r, k] - column[r] * column[k]
                upper[c] = upper[c] * root
                inverse[c] = inverse[c] * root
                for r in range(c + 1, eight):
                    upper[r] = upper[r] - column[r] * upper[c]
                    inverse[r] = inverse[r] - column[r] * inverse[c]
            for k in range(j + 1, rest):
                own = lane == sub + eight * k
                turned = [
                    jnp.sum(jnp.where(own, u, 0.0), axis=1, keepdims=True) for u in upper
                ]
                rows[k] = rows[k] - sum(t * u for t, u in zip(turned, upper))
                eyes[k] = eyes[k] - sum(t * v for t, v in zip(turned, inverse))
            uppers.append(join(upper))
            inverses.append(join(inverse))
        if rest < len(rows):
            u = jnp.concatenate(uppers[first:rest], axis=0)
            v = jnp.concatenate(inverses[first:rest], axis=0)
            below = u.T[eight * rest :]
            dot = functools.partial(
                jnp.dot, precision=lax.Precision.HIGHEST, preferred_element_type=F32
            )
            du, dv = dot(below, u), dot(below, v)
            for k in range(rest, len(rows)):
                o = slice(eight * (k - rest), eight * (k - rest + 1))
                rows[k] = rows[k] - du[o]
                eyes[k] = eyes[k] - dv[o]
    return jnp.concatenate(uppers, axis=0), jnp.concatenate(inverses, axis=0)


def modes_kernel(places, scale, gram_ref, more_ref, *rest):
    n = len(rest) - 7
    sources, (out, lower_ref, held, made, rows, in_sems, out_sems) = rest[:n], rest[n:]
    snaps, comps, _, cells_y, cells_z = out.shape
    width = cells_y * cells_z

    def reads(x):
        copies, lane = [], 0
        for m, (source, layer, count) in enumerate(places[x]):
            lanes = pl.ds(lane, count * width)
            lane += count * width
            copies.append(
                pltpu.make_async_copy(
                    sources[source].at[layer], held.at[x, :, lanes], in_sems.at[x, m]
                )
            )
        return copies

    for x in range(len(places)):
        for copy in reads(x):
            copy.start()

    upper, inverse = factorize(
        [
            (gram_ref[r : r + 8, :] + more_ref[r : r + 8, :]) * scale
            for r in range(0, snaps, 8)
        ],
        4,
    )
    r = lax.broadcasted_iota(jnp.int32, (snaps, snaps), 0)
    c = lax.broadcasted_iota(jnp.int32, (snaps, snaps), 1)
    lower_ref[...] = jnp.where(r >= c, upper.T, 0.0)
    inverse = inverse.astype(BF16)

    writes = []
    for x in range(len(places)):
        for copy in reads(x):
            copy.wait()
        for f in range(comps):
            lanes = slice(f * width, (f + 1) * width)
            whole = jnp.dot(inverse, held[x, :, lanes], preferred_element_type=F32)
            for y in range(cells_y):
                rows[f % 2, pl.ds(y, snaps, stride=PITCH), :] = whole[
                    :, y * cells_z : (y + 1) * cells_z
                ]
            for s in range(snaps):
                made[x, s, f] = rows[f % 2, pl.ds(s * PITCH, cells_y), :].astype(BF16)
        writes.append(pltpu.make_async_copy(made.at[x], out.at[:, :, x], out_sems.at[x]))
        writes[-1].start()
    for w in writes:
        w.wait()


def modes(gram, more, scale, sources, places, cells_y, cells_z):
    snaps = gram.shape[0]
    cells_x = len(places)
    return pl.pallas_call(
        functools.partial(modes_kernel, places, scale),
        in_specs=[VMEM, VMEM] + [HBM] * len(sources),
        out_specs=[HBM, VMEM],
        out_shape=[
            jax.ShapeDtypeStruct((snaps, 4, cells_x, cells_y, cells_z), BF16),
            jax.ShapeDtypeStruct((snaps, snaps), F32),
        ],
        scratch_shapes=[
            pltpu.VMEM((cells_x, snaps, 4 * cells_y * cells_z), BF16),
            pltpu.VMEM((cells_x, snaps, 4, cells_y, cells_z), BF16),
            pltpu.VMEM((2, snaps * PITCH, cells_z), F32),
            DMA((cells_x, 2)),
            DMA((cells_x,)),
        ],
        compiler_params=limit(32),
    )(gram, more, *sources)


def total(local):
    steps = []
    for axis in ("cross", "stream"):
        count = lax.axis_size(axis)
        steps += [(axis, count, 1 << k) for k in range((count - 1).bit_length())]
    more = jnp.zeros_like(local)
    for axis, count, step in steps:
        local = local + more
        more = lax.ppermute(local, axis, [(i, i ^ step) for i in range(count)])
    return local, more


def shift(cells, axis, way):
    count = lax.axis_size(axis)
    pairs = [(i, i + way) for i in range(count) if 0 <= i + way < count]
    return lax.ppermute(cells, axis, pairs)


def both_ways(pairs):
    return [p for a, b in pairs for p in ((a, b), (b, a))]


def far_exchange(far2):
    count = lax.axis_size("stream")
    direct = both_ways([(i, i + 1) for i in range(1, count - 1, 2)])
    if count == 4:
        half_way = lax.ppermute(far2, "stream", [(1, 3), (2, 0)])
        return half_way, lambda cells: lax.ppermute(cells, "stream", [(3, 2), (0, 1)]), direct
    return far2, lambda cells: lax.ppermute(cells, "stream", direct), direct


def shards(velocity, metric_x, metric_y, metric_z):
    snaps, comps, cells_x, cells_y, cells_z = velocity.shape
    count = lax.axis_size("stream")
    near, far1, far2, first, last = edges(velocity)
    after_edges, _ = lax.optimization_barrier((velocity, near))
    half_way, second_hop, direct = far_exchange(far2)
    near = lax.ppermute(near, "stream", both_ways([(i, i + 1) for i in range(0, count - 1, 2)]))
    far1 = lax.ppermute(far1, "stream", direct)
    low = shift(last, "cross", 1)
    high = shift(first, "cross", -1)
    cells = planes(after_edges)
    half_way, cells = lax.optimization_barrier((half_way, cells))
    far2 = second_hop(half_way)

    taps = jnp.zeros((cells_z, cells_z), F32)
    for step, weight in ((1, 8.0), (-1, -8.0), (2, -1.0), (-2, 1.0)):
        taps = taps + weight * jnp.eye(cells_z, k=-step, dtype=F32)
    metrics = (metric_x / 12.0, metric_y / 12.0, metric_z[None, :] / 12.0, taps.astype(BF16))
    middle, ends, parts, gram = inner_fields(cells, low, high, metrics)
    outer, gram = outer_fields(metrics[0], gram, parts, near, far1, far2)
    everywhere = (
        4.0 * cells_x * lax.axis_size("stream") * cells_y * lax.axis_size("cross") * cells_z
    )
    gram, more = total(gram)
    end = lambda x: x if x < 2 else x - cells_x + 4
    places = [
        [(0, x - 2, 4)] if 2 <= x < cells_x - 2 else [(1, end(x), 1), (2, end(x), 3)]
        for x in range(cells_x)
    ]
    sources = [middle, ends, outer]
    return tuple(modes(gram, more, 1.0 / everywhere, sources, places, cells_y, cells_z))


def solution(mesh):
    return jax.shard_map(
        shards,
        mesh=mesh,
        in_specs=(P(None, None, "stream", "cross", None), P("stream"), P("cross"), P()),
        out_specs=(P(None, None, "stream", "cross", None), P()),
        check_vma=False,
    )
```

```python
import functools

import jax
import jax.numpy as jnp
from jax import lax
from jax.experimental import pallas as pl
from jax.experimental.pallas import tpu as pltpu
from jax.sharding import PartitionSpec as P

F32, BF16 = jnp.float32, jnp.bfloat16
PITCH = 9
ROWS = 16
SLOTS = 4
HBM = pl.BlockSpec(memory_space=pl.ANY)
SMEM = pl.BlockSpec(memory_space=pltpu.SMEM)
VMEM = pl.BlockSpec(memory_space=pltpu.VMEM)
DMA = pltpu.SemaphoreType.DMA


def limit(mib):
    return pltpu.CompilerParams(vmem_limit_bytes=mib * 1024 * 1024)


def turn(tile, rows, ys, put):
    snaps, cells_y, cells_z = tile.shape
    wide = tile.astype(F32)
    for s in range(snaps):
        rows[pl.ds(s * PITCH, cells_y), :] = wide[s]
    for y in ys:
        put(y, rows[pl.ds(y, snaps, stride=PITCH), :].astype(BF16))


def edges_kernel(
    velocity, near, far1, far2, first, last, tiles, inner, ends, sides, rows, *sems
):
    end_in, inner_in, end_out, side_out = sems
    snaps, comps, cells_x, cells_y, _ = velocity.shape
    odd = lax.rem(lax.axis_index("stream"), 2)
    firsts = ((1 - odd) * (cells_x - 2), odd * (cells_x - 2))
    half = cells_y // 2
    between = cells_x - 4
    order = [(side, c) for side in (1, 0) for c in range(comps)]

    def end_read(side, c):
        return pltpu.make_async_copy(
            velocity.at[:, c, pl.ds(firsts[side], 2)], tiles.at[side, c], end_in.at[side, c]
        )

    def inner_read(c):
        return pltpu.make_async_copy(
            velocity.at[:, c, pl.ds(2, between)], inner.at[c], inner_in.at[c]
        )

    def side_writes(c, x):
        return [
            pltpu.make_async_copy(sides.at[k, c, x], ref.at[c, x], side_out.at[k, c, x])
            for k, ref in enumerate((first, last))
        ]

    def put_side(c, x, y, plane):
        if y < 2:
            sides[0, c, x, y] = plane
        elif y >= cells_y - 2:
            sides[1, c, x, y - cells_y + 2] = plane

    for side, c in order:
        end_read(side, c).start()
    for c in range(comps):
        inner_read(c).start()
    writes = []
    for side, c in order:
        end_read(side, c).wait()

        def one_end(layer, _):
            x = firsts[side] + layer

            def put(y, plane):
                ends[side, c, layer, y] = plane
                put_side(c, x, y, plane)

            turn(tiles[side, c, :, layer], rows, range(cells_y), put)
            for w in side_writes(c, x):
                w.start()
            return 0

        lax.fori_loop(0, 2, one_end, 0)
        if side == 0:
            parts = [(ends.at[0, c], near.at[c])]
        else:
            parts = [
                (ends.at[1, c, :, pl.ds(0, half)], far1.at[c]),
                (ends.at[1, c, :, pl.ds(half, half)], far2.at[c]),
            ]
        for src, dst in parts:
            writes.append(pltpu.make_async_copy(src, dst, end_out.at[len(writes)]))
            writes[-1].start()

    for c in range(comps):
        inner_read(c).wait()

        def one_inner(n, _):
            turn(
                inner[c, :, n],
                rows,
                (0, 1, cells_y - 2, cells_y - 1),
                functools.partial(put_side, c, n + 2),
            )
            for w in side_writes(c, n + 2):
                w.start()
            return 0

        lax.fori_loop(0, between, one_inner, 0)

    for w in writes:
        w.wait()

    def finish(n, _):
        for w in side_writes(n // cells_x, lax.rem(n, cells_x)):
            w.wait()
        return 0

    lax.fori_loop(0, comps * cells_x, finish, 0)


def edges(velocity):
    snaps, comps, cells_x, cells_y, cells_z = velocity.shape
    shape = lambda layers, rows: jax.ShapeDtypeStruct((comps, layers, rows, snaps, cells_z), BF16)
    return pl.pallas_call(
        edges_kernel,
        in_specs=[HBM],
        out_specs=[HBM] * 5,
        out_shape=[shape(2, cells_y)] + [shape(2, cells_y // 2)] * 2 + [shape(cells_x, 2)] * 2,
        scratch_shapes=[
            pltpu.VMEM((2, comps, snaps, 2, cells_y, cells_z), BF16),
            pltpu.VMEM((comps, snaps, cells_x - 4, cells_y, cells_z), BF16),
            pltpu.VMEM((2, comps, 2, cells_y, snaps, cells_z), BF16),
            pltpu.VMEM((2, comps, cells_x, 2, snaps, cells_z), BF16),
            pltpu.VMEM((snaps * PITCH, cells_z), F32),
            DMA((2, comps)),
            DMA((comps,)),
            DMA((3 * comps,)),
            DMA((2, comps, cells_x)),
        ],
        compiler_params=limit(60),
    )(velocity)


def planes_kernel(velocity, cells, taken, turned, rows, in_sems, out_sems):
    snaps, comps, cells_x, cells_y, cells_z = velocity.shape

    def read(c, x):
        return pltpu.make_async_copy(velocity.at[:, c, x], taken.at[c, x], in_sems.at[c, x])

    def write(c, x):
        return pltpu.make_async_copy(turned.at[c, x], cells.at[c, x], out_sems.at[c, x])

    def each(work):
        def step(n, _):
            work(n // cells_x, lax.rem(n, cells_x))
            return 0

        lax.fori_loop(0, comps * cells_x, step, 0)

    def one(c, x):
        read(c, x).wait()

        def put(y, plane):
            turned[c, x, y] = plane

        turn(taken[c, x], rows, range(cells_y), put)
        write(c, x).start()

    each(lambda c, x: read(c, x).start())
    each(one)
    each(lambda c, x: write(c, x).wait())


def planes(velocity):
    snaps, comps, cells_x, cells_y, cells_z = velocity.shape
    return pl.pallas_call(
        planes_kernel,
        in_specs=[HBM],
        out_specs=HBM,
        out_shape=jax.ShapeDtypeStruct((comps, cells_x, cells_y, snaps, cells_z), BF16),
        scratch_shapes=[
            pltpu.VMEM((comps, cells_x, snaps, cells_y, cells_z), BF16),
            pltpu.VMEM((comps, cells_x, cells_y, snaps, cells_z), BF16),
            pltpu.VMEM((snaps * PITCH, cells_z), F32),
            DMA((comps, cells_x)),
            DMA((comps, cells_x)),
        ],
        compiler_params=limit(60),
    )(velocity)


def layer_fields(ring, slots, rz, low, high, metric_x, metric_y_ref, metric_z, puts):
    cells_y, snaps, cells_z = ring.shape[2:]
    back2, back1, here, fore1, fore2 = slots

    def some_rows(step, _):
        at = pl.ds(pl.multiple_of(step * ROWS, ROWS), ROWS)

        def row(comp, y):
            if y < 0:
                return low[comp, y + 2, at, :].astype(F32)
            if y >= cells_y:
                return high[comp, y - cells_y, at, :].astype(F32)
            return ring[here, comp, y, at, :]

        window = [[row(c, y) for y in range(-2, 2)] for c in range(3)]
        for y in range(cells_y):
            for c in range(3):
                window[c].append(row(c, y + 2))

            def along_x(c):
                near = ring[fore1, c, y, at, :] - ring[back1, c, y, at, :]
                far = ring[fore2, c, y, at, :] - ring[back2, c, y, at, :]
                return (8.0 * near - far) * metric_x

            def along_y(c):
                w = window[c]
                return (8.0 * (w[3] - w[1]) - (w[4] - w[0])) * metric_y_ref[y]

            def along_z(c):
                return rz[c, y, at, :] * metric_z

            puts[0](at, y, along_y(2) - along_z(1))
            puts[1](at, y, along_z(0) - along_x(2))
            puts[2](at, y, along_x(1) - along_y(0))
            puts[3](at, y, along_x(0) + along_y(1) + along_z(2))
            for c in range(3):
                window[c] = window[c][1:]
        return 0

    lax.fori_loop(0, snaps // ROWS, some_rows, 0, unroll=2)


def inner_kernel(mx_ref, my_ref, mz_ref, taps_ref, cells, low, high, *rest):
    middle, ends, parts, gram_ref = rest[:4]
    layers, lows, highs, ring, rz_ring, done, done_ends, done_parts, in_sems, out_sems = rest[4:]
    comps, cells_y, snaps, cells_z = ring.shape[1:]
    cells_x = lows.shape[0]
    width = cells_y * cells_z

    def reads(x):
        return [
            pltpu.make_async_copy(cells.at[:, x], layers.at[x % SLOTS], in_sems.at[0, x]),
            pltpu.make_async_copy(low.at[:, x], lows.at[x], in_sems.at[1, x]),
            pltpu.make_async_copy(high.at[:, x], highs.at[x], in_sems.at[2, x]),
        ]

    def put_in(ref, lane):
        def put(at, y, value):
            ref[at, lane + y * cells_z : lane + (y + 1) * cells_z] = value.astype(ref.dtype)

        return put

    for x in range(SLOTS):
        for copy in reads(x):
            copy.start()
    gram_ref[...] = jnp.zeros_like(gram_ref)
    writes, middle_writes = [], []

    def write(src, dst):
        sem = out_sems.at[len(writes) + len(middle_writes)]
        writes.append(pltpu.make_async_copy(src, dst, sem))
        writes[-1].start()

    for i in range(cells_x + 4):
        if 2 <= i < cells_x + 2:
            for copy in reads(i - 2):
                copy.wait()
            slot = layers.at[(i - 2) % SLOTS]
            ring[i % 5] = slot[...].astype(F32)
            flat = slot[...].reshape(comps * cells_y * snaps, cells_z)
            rz_ring[i % 3] = jnp.dot(flat, taps_ref[...], preferred_element_type=F32).reshape(
                comps, cells_y, snaps, cells_z
            )
            if i - 2 + SLOTS < cells_x:
                for copy in reads(i - 2 + SLOTS):
                    copy.start()
        else:
            ring[i % 5] = jnp.zeros(ring.shape[1:], F32)
        x = i - 4
        if x < 0:
            continue
        is_inner = 2 <= x < cells_x - 2
        e = x if x < 2 else x - cells_x + 4
        if is_inner:
            made = done.at[x % SLOTS]
            if x - 2 >= SLOTS:
                middle_writes[x - 2 - SLOTS].wait()
            puts = [put_in(made, f * width) for f in range(4)]
        else:
            made = done_ends.at[e]
            puts = [put_in(made, 0)]
            puts += [put_in(done_parts.at[e], f * width) for f in range(3)]
        layer_fields(
            ring,
            [(i + 1 + s) % 5 for s in range(5)],
            rz_ring.at[(i - 2) % 3],
            lows.at[x],
            highs.at[x],
            mx_ref[x],
            my_ref,
            mz_ref[...],
            puts,
        )
        if is_inner:
            write(made, middle.at[x - 2])
            middle_writes.append(writes.pop())
        else:
            write(made, ends.at[e])
            write(done_parts.at[e], parts.at[e])
        gram_ref[...] += lax.dot_general(
            made[...], made[...], (((1,), (1,)), ((), ())), preferred_element_type=F32
        )
    for w in writes + middle_writes[-SLOTS:]:
        w.wait()


def inner_fields(cells, low, high, metrics):
    comps, cells_x, cells_y, snaps, cells_z = cells.shape
    width = cells_y * cells_z
    return pl.pallas_call(
        inner_kernel,
        in_specs=[SMEM, SMEM, VMEM, VMEM] + [HBM] * 3,
        out_specs=[HBM] * 3 + [VMEM],
        out_shape=[
            jax.ShapeDtypeStruct((cells_x - 4, snaps, 4 * width), BF16),
            jax.ShapeDtypeStruct((4, snaps, width), BF16),
            jax.ShapeDtypeStruct((4, snaps, 3 * width), F32),
            jax.ShapeDtypeStruct((snaps, snaps), F32),
        ],
        scratch_shapes=[
            pltpu.VMEM((SLOTS, comps, cells_y, snaps, cells_z), BF16),
            pltpu.VMEM((cells_x, comps, 2, snaps, cells_z), BF16),
            pltpu.VMEM((cells_x, comps, 2, snaps, cells_z), BF16),
            pltpu.VMEM((5, comps, cells_y, snaps, cells_z), F32),
            pltpu.VMEM((3, comps, cells_y, snaps, cells_z), F32),
            pltpu.VMEM((SLOTS, snaps, 4 * width), BF16),
            pltpu.VMEM((4, snaps, width), BF16),
            pltpu.VMEM((4, snaps, 3 * width), F32),
            DMA((3, cells_x)),
            DMA((cells_x + 4,)),
        ],
        compiler_params=limit(36),
    )(*metrics, cells, low, high)


def triangle(whole):
    n = whole.shape[0]
    half = n // 2
    r = lax.broadcasted_iota(jnp.int32, (half, n), 0)
    c = lax.broadcasted_iota(jnp.int32, (half, n), 1)
    top, bottom = whole[:half], whole[half:]
    packed = jnp.where(c - half <= r, bottom, pltpu.roll(top, half, 1))
    diagonal = jnp.sum(jnp.where(r == c, top, 0.0), axis=0, keepdims=True)
    return packed, jnp.broadcast_to(diagonal, (8, n))


def symmetric(packed):
    n = packed.shape[1]
    half = n // 2
    r = lax.broadcasted_iota(jnp.int32, (half, n), 0)
    c = lax.broadcasted_iota(jnp.int32, (half, n), 1)
    rows, diagonal = packed[:half], packed[half : half + 1]
    top = jnp.where((c > r) & (c < half), pltpu.roll(rows, half, 1), 0.0)
    top = jnp.where(r == c, jnp.broadcast_to(diagonal, (half, n)), top)
    one = jnp.concatenate([top, jnp.where(c - half <= r, rows, 0.0)], axis=0)
    r = lax.broadcasted_iota(jnp.int32, (n, n), 0)
    c = lax.broadcasted_iota(jnp.int32, (n, n), 1)
    return jnp.where(r == c, one, one + one.T)


def outer_kernel(near, far1, far2, parts, mx_ref, gram_ref, out, total_ref, *rest):
    taken, halos, done, part_sems, halo_sems, out_sems = rest
    _, comps, _, cells_y, snaps, cells_z = halos.shape
    half = cells_y // 2
    width = cells_y * cells_z
    cells_x = mx_ref.shape[0]
    odd = lax.rem(lax.axis_index("stream"), 2)

    def part_read(e):
        return pltpu.make_async_copy(parts.at[e], taken.at[e], part_sems.at[e])

    def halo_reads(side, run):
        sem = halo_sems.at[side]
        is_near = (odd == 1) == (side == 0)
        first, second = pl.ds(0, half), pl.ds(half, half)

        @pl.when(is_near)
        def _():
            run(pltpu.make_async_copy(near, halos.at[side], sem.at[0]))

        @pl.when(jnp.logical_not(is_near))
        def _():
            run(pltpu.make_async_copy(far1, halos.at[side, :, :, first], sem.at[0]))
            run(pltpu.make_async_copy(far2, halos.at[side, :, :, second], sem.at[1]))

    for side in range(2):
        halo_reads(side, lambda copy: copy.start())
        for e in (2 * side, 2 * side + 1):
            part_read(e).start()
    total = gram_ref[...]
    writes = []
    last = cells_x - 1
    plan = (
        (0, 0, 0, (1.0, -8.0)),
        (1, 1, 0, (0.0, 1.0)),
        (2, last - 1, 1, (-1.0, 0.0)),
        (3, last, 1, (8.0, -1.0)),
    )
    for e, x, side, weights in plan:
        if e % 2 == 0:
            halo_reads(side, lambda copy: copy.wait())
        part_read(e).wait()
        metric_x = mx_ref[x]

        def some_rows(step, _):
            at = pl.ds(pl.multiple_of(step * ROWS, ROWS), ROWS)
            for f, (comp, sign) in enumerate(((2, -1.0), (1, 1.0), (0, 1.0))):
                for y in range(cells_y):
                    lanes = slice(f * width + y * cells_z, f * width + (y + 1) * cells_z)
                    sums = [
                        (sign * w) * halos[side, comp, k, y, at, :].astype(F32)
                        for k, w in enumerate(weights)
                        if w
                    ]
                    value = taken[e, at, lanes] + functools.reduce(jnp.add, sums) * metric_x
                    done[e, at, lanes] = value.astype(BF16)
            return 0

        lax.fori_loop(0, snaps // ROWS, some_rows, 0)
        writes.append(pltpu.make_async_copy(done.at[e], out.at[e], out_sems.at[e]))
        writes[-1].start()
        total += lax.dot_general(
            done[e], done[e], (((1,), (1,)), ((), ())), preferred_element_type=F32
        )
    half = snaps // 2
    total_ref[:half], total_ref[half:] = triangle(total)
    for w in writes:
        w.wait()


def outer_fields(metric_x, gram, parts, near, far1, far2):
    comps, _, cells_y, snaps, cells_z = near.shape
    lanes = parts.shape[2]
    return pl.pallas_call(
        outer_kernel,
        in_specs=[HBM] * 4 + [SMEM, VMEM],
        out_specs=[HBM, VMEM],
        out_shape=[
            jax.ShapeDtypeStruct(parts.shape, BF16),
            jax.ShapeDtypeStruct((snaps // 2 + 8, snaps), F32),
        ],
        scratch_shapes=[
            pltpu.VMEM(parts.shape, F32),
            pltpu.VMEM((2, comps, 2, cells_y, snaps, cells_z), BF16),
            pltpu.VMEM(parts.shape, BF16),
            DMA((4,)),
            DMA((2, 2)),
            DMA((4,)),
        ],
        compiler_params=limit(20),
    )(near, far1, far2, parts, metric_x, gram)


def factorize(rows, panel):
    eight, n = rows[0].shape
    shape = (eight, n)
    sub = lax.broadcasted_iota(jnp.int32, shape, 0)
    lane = lax.broadcasted_iota(jnp.int32, shape, 1)
    rows = list(rows)
    eyes = [jnp.where(lane == sub + eight * j, 1.0, 0.0).astype(F32) for j in range(len(rows))]
    uppers, inverses = [], []

    def spread(block, r):
        return jnp.broadcast_to(block[r : r + 1], shape)

    def join(parts):
        out = parts[0]
        for r in range(1, eight):
            out = jnp.where(sub == r, parts[r], out)
        return out

    for first in range(0, len(rows), panel):
        rest = first + panel
        for j in range(first, rest):
            at = eight * j
            left = {
                (r, c): jnp.broadcast_to(rows[j][r : r + 1, at + c : at + c + 1], shape)
                for r in range(eight)
                for c in range(r + 1)
            }
            upper = [spread(rows[j], r) for r in range(eight)]
            inverse = [spread(eyes[j], r) for r in range(eight)]
            for c in range(eight):
                root = lax.rsqrt(left[c, c])
                column = {r: left[r, c] * root for r in range(c + 1, eight)}
                for k in range(c + 1, eight):
                    for r in range(k, eight):
                        left[r, k] = left[r, k] - column[r] * column[k]
                upper[c] = upper[c] * root
                inverse[c] = inverse[c] * root
                for r in range(c + 1, eight):
                    upper[r] = upper[r] - column[r] * upper[c]
                    inverse[r] = inverse[r] - column[r] * inverse[c]
            for k in range(j + 1, rest):
                own = lane == sub + eight * k
                turned = [
                    jnp.sum(jnp.where(own, u, 0.0), axis=1, keepdims=True) for u in upper
                ]
                rows[k] = rows[k] - sum(t * u for t, u in zip(turned, upper))
                eyes[k] = eyes[k] - sum(t * v for t, v in zip(turned, inverse))
            uppers.append(join(upper))
            inverses.append(join(inverse))
        if rest < len(rows):
            u = jnp.concatenate(uppers[first:rest], axis=0)
            v = jnp.concatenate(inverses[first:rest], axis=0)
            below = u.T[eight * rest :]
            dot = functools.partial(
                jnp.dot, precision=lax.Precision.HIGHEST, preferred_element_type=F32
            )
            du, dv = dot(below, u), dot(below, v)
            for k in range(rest, len(rows)):
                o = slice(eight * (k - rest), eight * (k - rest + 1))
                rows[k] = rows[k] - du[o]
                eyes[k] = eyes[k] - dv[o]
    return jnp.concatenate(uppers, axis=0), jnp.concatenate(inverses, axis=0)


def modes_kernel(places, scale, n_terms, *rest):
    terms, rest = rest[:n_terms], rest[n_terms:]
    n = len(rest) - 7
    sources, (out, lower_ref, held, made, rows, in_sems, out_sems) = rest[:n], rest[n:]
    snaps, comps, _, cells_y, cells_z = out.shape
    width = cells_y * cells_z

    def reads(x):
        copies, lane = [], 0
        for m, (source, layer, count) in enumerate(places[x]):
            lanes = pl.ds(lane, count * width)
            lane += count * width
            copies.append(
                pltpu.make_async_copy(
                    sources[source].at[layer], held.at[x, :, lanes], in_sems.at[x, m]
                )
            )
        return copies

    for x in range(len(places)):
        for copy in reads(x):
            copy.start()

    gram = symmetric(tree_sum([term[...] for term in terms]) * scale)
    upper, inverse = factorize([gram[r : r + 8] for r in range(0, snaps, 8)], 4)
    r = lax.broadcasted_iota(jnp.int32, (snaps, snaps), 0)
    c = lax.broadcasted_iota(jnp.int32, (snaps, snaps), 1)
    lower_ref[...] = jnp.where(r >= c, upper.T, 0.0)
    inverse = inverse.astype(BF16)

    writes = []
    for x in range(len(places)):
        for copy in reads(x):
            copy.wait()
        for f in range(comps):
            lanes = slice(f * width, (f + 1) * width)
            whole = jnp.dot(inverse, held[x, :, lanes], preferred_element_type=F32)
            for y in range(cells_y):
                rows[f % 2, pl.ds(y, snaps, stride=PITCH), :] = whole[
                    :, y * cells_z : (y + 1) * cells_z
                ]
            for s in range(snaps):
                made[x, s, f] = rows[f % 2, pl.ds(s * PITCH, cells_y), :].astype(BF16)
        writes.append(pltpu.make_async_copy(made.at[x], out.at[:, :, x], out_sems.at[x]))
        writes[-1].start()
    for w in writes:
        w.wait()


def modes(terms, scale, sources, places, cells_y, cells_z):
    snaps = terms[0].shape[1]
    cells_x = len(places)
    return pl.pallas_call(
        functools.partial(modes_kernel, places, scale, len(terms)),
        in_specs=[VMEM] * len(terms) + [HBM] * len(sources),
        out_specs=[HBM, VMEM],
        out_shape=[
            jax.ShapeDtypeStruct((snaps, 4, cells_x, cells_y, cells_z), BF16),
            jax.ShapeDtypeStruct((snaps, snaps), F32),
        ],
        scratch_shapes=[
            pltpu.VMEM((cells_x, snaps, 4 * cells_y * cells_z), BF16),
            pltpu.VMEM((cells_x, snaps, 4, cells_y, cells_z), BF16),
            pltpu.VMEM((2, snaps * PITCH, cells_z), F32),
            DMA((cells_x, 2)),
            DMA((cells_x,)),
        ],
        compiler_params=limit(32),
    )(*terms, *sources)


def tree_sum(terms):
    while len(terms) > 1:
        terms = [terms[i] + terms[i + 1] for i in range(0, len(terms), 2)]
    return terms[0]


def exchange(local):
    groups = []
    for axis in ("cross", "stream"):
        count = lax.axis_size(axis)
        bits = [1 << k for k in range((count - 1).bit_length())]
        if axis == "cross":
            groups, bits = groups + [(axis, count, bits[:1])], bits[1:]
        groups += [(axis, count, bits[k : k + 2]) for k in range(0, len(bits), 2)]
    terms = [local]
    for axis, count, bits in groups:
        local = tree_sum(terms)
        steps = [sum(b for k, b in enumerate(bits) if n >> k & 1) for n in range(1 << len(bits))]
        terms = [local] + [
            lax.ppermute(local, axis, [(i, i ^ step) for i in range(count)]) for step in steps[1:]
        ]
    return terms


def shift(cells, axis, way):
    count = lax.axis_size(axis)
    pairs = [(i, i + way) for i in range(count) if 0 <= i + way < count]
    return lax.ppermute(cells, axis, pairs)


def both_ways(pairs):
    return [p for a, b in pairs for p in ((a, b), (b, a))]


def far_exchange(far2):
    count = lax.axis_size("stream")
    direct = both_ways([(i, i + 1) for i in range(1, count - 1, 2)])
    if count == 4:
        half_way = lax.ppermute(far2, "stream", [(1, 3), (2, 0)])
        return half_way, lambda cells: lax.ppermute(cells, "stream", [(3, 2), (0, 1)]), direct
    return far2, lambda cells: lax.ppermute(cells, "stream", direct), direct


def shards(velocity, metric_x, metric_y, metric_z):
    snaps, comps, cells_x, cells_y, cells_z = velocity.shape
    count = lax.axis_size("stream")
    near, far1, far2, first, last = edges(velocity)
    after_edges, _ = lax.optimization_barrier((velocity, near))
    half_way, second_hop, direct = far_exchange(far2)
    near = lax.ppermute(near, "stream", both_ways([(i, i + 1) for i in range(0, count - 1, 2)]))
    far1 = lax.ppermute(far1, "stream", direct)
    low = shift(last, "cross", 1)
    high = shift(first, "cross", -1)
    cells = planes(after_edges)
    half_way, cells = lax.optimization_barrier((half_way, cells))
    far2 = second_hop(half_way)

    taps = jnp.zeros((cells_z, cells_z), F32)
    for step, weight in ((1, 8.0), (-1, -8.0), (2, -1.0), (-2, 1.0)):
        taps = taps + weight * jnp.eye(cells_z, k=-step, dtype=F32)
    metrics = (metric_x / 12.0, metric_y / 12.0, metric_z[None, :] / 12.0, taps.astype(BF16))
    middle, ends, parts, gram = inner_fields(cells, low, high, metrics)
    outer, gram = outer_fields(metrics[0], gram, parts, near, far1, far2)
    everywhere = (
        4.0 * cells_x * lax.axis_size("stream") * cells_y * lax.axis_size("cross") * cells_z
    )
    terms = exchange(gram)
    end = lambda x: x if x < 2 else x - cells_x + 4
    places = [
        [(0, x - 2, 4)] if 2 <= x < cells_x - 2 else [(1, end(x), 1), (2, end(x), 3)]
        for x in range(cells_x)
    ]
    sources = [middle, ends, outer]
    return tuple(modes(terms, 1.0 / everywhere, sources, places, cells_y, cells_z))


def solution(mesh):
    return jax.shard_map(
        shards,
        mesh=mesh,
        in_specs=(P(None, None, "stream", "cross", None), P("stream"), P("cross"), P()),
        out_specs=(P(None, None, "stream", "cross", None), P()),
        check_vma=False,
    )
```

```python
import functools

import jax
import jax.numpy as jnp
from jax import lax
from jax.experimental import pallas as pl
from jax.experimental.pallas import tpu as pltpu
from jax.sharding import PartitionSpec as P

F32, BF16 = jnp.float32, jnp.bfloat16
PITCH = 9
ROWS = 16
SLOTS = 4
HBM = pl.BlockSpec(memory_space=pl.ANY)
SMEM = pl.BlockSpec(memory_space=pltpu.SMEM)
VMEM = pl.BlockSpec(memory_space=pltpu.VMEM)
DMA = pltpu.SemaphoreType.DMA


def limit(mib):
    return pltpu.CompilerParams(vmem_limit_bytes=mib * 1024 * 1024)


def turn(tile, rows, ys, put):
    snaps, cells_y, cells_z = tile.shape
    wide = tile.astype(F32)
    for s in range(snaps):
        rows[pl.ds(s * PITCH, cells_y), :] = wide[s]
    for y in ys:
        put(y, rows[pl.ds(y, snaps, stride=PITCH), :].astype(BF16))


def edges_kernel(
    velocity, near, far1, far2, first, last, tiles, inner, ends, sides, rows, *sems
):
    end_in, inner_in, end_out, side_out = sems
    snaps, comps, cells_x, cells_y, _ = velocity.shape
    odd = lax.rem(lax.axis_index("stream"), 2)
    firsts = ((1 - odd) * (cells_x - 2), odd * (cells_x - 2))
    half = cells_y // 2
    between = cells_x - 4
    order = [(side, c) for side in (1, 0) for c in range(comps)]

    def end_read(side, c):
        return pltpu.make_async_copy(
            velocity.at[:, c, pl.ds(firsts[side], 2)], tiles.at[side, c], end_in.at[side, c]
        )

    def inner_read(c):
        return pltpu.make_async_copy(
            velocity.at[:, c, pl.ds(2, between)], inner.at[c], inner_in.at[c]
        )

    def side_writes(c, x):
        return [
            pltpu.make_async_copy(sides.at[k, c, x], ref.at[c, x], side_out.at[k, c, x])
            for k, ref in enumerate((first, last))
        ]

    def put_side(c, x, y, plane):
        if y < 2:
            sides[0, c, x, y] = plane
        elif y >= cells_y - 2:
            sides[1, c, x, y - cells_y + 2] = plane

    for side, c in order:
        end_read(side, c).start()
    for c in range(comps):
        inner_read(c).start()
    writes = []
    for side, c in order:
        end_read(side, c).wait()

        def one_end(layer, _):
            x = firsts[side] + layer

            def put(y, plane):
                ends[side, c, layer, y] = plane
                put_side(c, x, y, plane)

            turn(tiles[side, c, :, layer], rows, range(cells_y), put)
            for w in side_writes(c, x):
                w.start()
            return 0

        lax.fori_loop(0, 2, one_end, 0)
        if side == 0:
            parts = [(ends.at[0, c], near.at[c])]
        else:
            parts = [
                (ends.at[1, c, :, pl.ds(0, half)], far1.at[c]),
                (ends.at[1, c, :, pl.ds(half, half)], far2.at[c]),
            ]
        for src, dst in parts:
            writes.append(pltpu.make_async_copy(src, dst, end_out.at[len(writes)]))
            writes[-1].start()

    for c in range(comps):
        inner_read(c).wait()

        def one_inner(n, _):
            turn(
                inner[c, :, n],
                rows,
                (0, 1, cells_y - 2, cells_y - 1),
                functools.partial(put_side, c, n + 2),
            )
            for w in side_writes(c, n + 2):
                w.start()
            return 0

        lax.fori_loop(0, between, one_inner, 0)

    for w in writes:
        w.wait()

    def finish(n, _):
        for w in side_writes(n // cells_x, lax.rem(n, cells_x)):
            w.wait()
        return 0

    lax.fori_loop(0, comps * cells_x, finish, 0)


def edges(velocity):
    snaps, comps, cells_x, cells_y, cells_z = velocity.shape
    shape = lambda layers, rows: jax.ShapeDtypeStruct((comps, layers, rows, snaps, cells_z), BF16)
    return pl.pallas_call(
        edges_kernel,
        in_specs=[HBM],
        out_specs=[HBM] * 5,
        out_shape=[shape(2, cells_y)] + [shape(2, cells_y // 2)] * 2 + [shape(cells_x, 2)] * 2,
        scratch_shapes=[
            pltpu.VMEM((2, comps, snaps, 2, cells_y, cells_z), BF16),
            pltpu.VMEM((comps, snaps, cells_x - 4, cells_y, cells_z), BF16),
            pltpu.VMEM((2, comps, 2, cells_y, snaps, cells_z), BF16),
            pltpu.VMEM((2, comps, cells_x, 2, snaps, cells_z), BF16),
            pltpu.VMEM((snaps * PITCH, cells_z), F32),
            DMA((2, comps)),
            DMA((comps,)),
            DMA((3 * comps,)),
            DMA((2, comps, cells_x)),
        ],
        compiler_params=limit(60),
    )(velocity)


def planes_kernel(velocity, cells, taken, turned, rows, in_sems, out_sems):
    snaps, comps, cells_x, cells_y, cells_z = velocity.shape

    def read(c, x):
        return pltpu.make_async_copy(velocity.at[:, c, x], taken.at[c, x], in_sems.at[c, x])

    def write(c, x):
        return pltpu.make_async_copy(turned.at[c, x], cells.at[c, x], out_sems.at[c, x])

    def each(work):
        def step(n, _):
            work(n // cells_x, lax.rem(n, cells_x))
            return 0

        lax.fori_loop(0, comps * cells_x, step, 0)

    def one(c, x):
        read(c, x).wait()

        def put(y, plane):
            turned[c, x, y] = plane

        turn(taken[c, x], rows, range(cells_y), put)
        write(c, x).start()

    each(lambda c, x: read(c, x).start())
    each(one)
    each(lambda c, x: write(c, x).wait())


def planes(velocity):
    snaps, comps, cells_x, cells_y, cells_z = velocity.shape
    return pl.pallas_call(
        planes_kernel,
        in_specs=[HBM],
        out_specs=HBM,
        out_shape=jax.ShapeDtypeStruct((comps, cells_x, cells_y, snaps, cells_z), BF16),
        scratch_shapes=[
            pltpu.VMEM((comps, cells_x, snaps, cells_y, cells_z), BF16),
            pltpu.VMEM((comps, cells_x, cells_y, snaps, cells_z), BF16),
            pltpu.VMEM((snaps * PITCH, cells_z), F32),
            DMA((comps, cells_x)),
            DMA((comps, cells_x)),
        ],
        compiler_params=limit(60),
    )(velocity)


def layer_fields(ring, slots, rz, low, high, metric_x, metric_y_ref, metric_z, puts):
    cells_y, snaps, cells_z = ring.shape[2:]
    back2, back1, here, fore1, fore2 = slots

    def some_rows(step, _):
        at = pl.ds(pl.multiple_of(step * ROWS, ROWS), ROWS)

        def row(comp, y):
            if y < 0:
                return low[comp, y + 2, at, :].astype(F32)
            if y >= cells_y:
                return high[comp, y - cells_y, at, :].astype(F32)
            return ring[here, comp, y, at, :]

        window = [[row(c, y) for y in range(-2, 2)] for c in range(3)]
        for y in range(cells_y):
            for c in range(3):
                window[c].append(row(c, y + 2))

            def along_x(c):
                near = ring[fore1, c, y, at, :] - ring[back1, c, y, at, :]
                far = ring[fore2, c, y, at, :] - ring[back2, c, y, at, :]
                return (8.0 * near - far) * metric_x

            def along_y(c):
                w = window[c]
                return (8.0 * (w[3] - w[1]) - (w[4] - w[0])) * metric_y_ref[y]

            def along_z(c):
                return rz[c, y, at, :] * metric_z

            puts[0](at, y, along_y(2) - along_z(1))
            puts[1](at, y, along_z(0) - along_x(2))
            puts[2](at, y, along_x(1) - along_y(0))
            puts[3](at, y, along_x(0) + along_y(1) + along_z(2))
            for c in range(3):
                window[c] = window[c][1:]
        return 0

    lax.fori_loop(0, snaps // ROWS, some_rows, 0, unroll=2)


def inner_kernel(mx_ref, my_ref, mz_ref, taps_ref, cells, low, high, *rest):
    middle, ends, parts, gram_ref = rest[:4]
    layers, lows, highs, ring, rz_ring, done, done_ends, done_parts, in_sems, out_sems = rest[4:]
    comps, cells_y, snaps, cells_z = ring.shape[1:]
    cells_x = lows.shape[0]
    width = cells_y * cells_z

    def reads(x):
        return [
            pltpu.make_async_copy(cells.at[:, x], layers.at[x % SLOTS], in_sems.at[0, x]),
            pltpu.make_async_copy(low.at[:, x], lows.at[x], in_sems.at[1, x]),
            pltpu.make_async_copy(high.at[:, x], highs.at[x], in_sems.at[2, x]),
        ]

    def put_in(ref, lane):
        def put(at, y, value):
            ref[at, lane + y * cells_z : lane + (y + 1) * cells_z] = value.astype(ref.dtype)

        return put

    for x in range(SLOTS):
        for copy in reads(x):
            copy.start()
    gram_ref[...] = jnp.zeros_like(gram_ref)
    writes, middle_writes = [], []

    def write(src, dst):
        sem = out_sems.at[len(writes) + len(middle_writes)]
        writes.append(pltpu.make_async_copy(src, dst, sem))
        writes[-1].start()

    for i in range(cells_x + 4):
        if 2 <= i < cells_x + 2:
            for copy in reads(i - 2):
                copy.wait()
            slot = layers.at[(i - 2) % SLOTS]
            ring[i % 5] = slot[...].astype(F32)
            flat = slot[...].reshape(comps * cells_y * snaps, cells_z)
            rz_ring[i % 3] = jnp.dot(flat, taps_ref[...], preferred_element_type=F32).reshape(
                comps, cells_y, snaps, cells_z
            )
            if i - 2 + SLOTS < cells_x:
                for copy in reads(i - 2 + SLOTS):
                    copy.start()
        else:
            ring[i % 5] = jnp.zeros(ring.shape[1:], F32)
        x = i - 4
        if x < 0:
            continue
        is_inner = 2 <= x < cells_x - 2
        e = x if x < 2 else x - cells_x + 4
        if is_inner:
            made = done.at[x % SLOTS]
            if x - 2 >= SLOTS:
                middle_writes[x - 2 - SLOTS].wait()
            puts = [put_in(made, f * width) for f in range(4)]
        else:
            made = done_ends.at[e]
            puts = [put_in(made, 0)]
            puts += [put_in(done_parts.at[e], f * width) for f in range(3)]
        layer_fields(
            ring,
            [(i + 1 + s) % 5 for s in range(5)],
            rz_ring.at[(i - 2) % 3],
            lows.at[x],
            highs.at[x],
            mx_ref[x],
            my_ref,
            mz_ref[...],
            puts,
        )
        if is_inner:
            write(made, middle.at[x - 2])
            middle_writes.append(writes.pop())
        else:
            write(made, ends.at[e])
            write(done_parts.at[e], parts.at[e])
        gram_ref[...] += lax.dot_general(
            made[...], made[...], (((1,), (1,)), ((), ())), preferred_element_type=F32
        )
    for w in writes + middle_writes[-SLOTS:]:
        w.wait()


def inner_fields(cells, low, high, metrics):
    comps, cells_x, cells_y, snaps, cells_z = cells.shape
    width = cells_y * cells_z
    return pl.pallas_call(
        inner_kernel,
        in_specs=[SMEM, SMEM, VMEM, VMEM] + [HBM] * 3,
        out_specs=[HBM] * 3 + [VMEM],
        out_shape=[
            jax.ShapeDtypeStruct((cells_x - 4, snaps, 4 * width), BF16),
            jax.ShapeDtypeStruct((4, snaps, width), BF16),
            jax.ShapeDtypeStruct((4, snaps, 3 * width), F32),
            jax.ShapeDtypeStruct((snaps, snaps), F32),
        ],
        scratch_shapes=[
            pltpu.VMEM((SLOTS, comps, cells_y, snaps, cells_z), BF16),
            pltpu.VMEM((cells_x, comps, 2, snaps, cells_z), BF16),
            pltpu.VMEM((cells_x, comps, 2, snaps, cells_z), BF16),
            pltpu.VMEM((5, comps, cells_y, snaps, cells_z), F32),
            pltpu.VMEM((3, comps, cells_y, snaps, cells_z), F32),
            pltpu.VMEM((SLOTS, snaps, 4 * width), BF16),
            pltpu.VMEM((4, snaps, width), BF16),
            pltpu.VMEM((4, snaps, 3 * width), F32),
            DMA((3, cells_x)),
            DMA((cells_x + 4,)),
        ],
        compiler_params=limit(36),
    )(*metrics, cells, low, high)


def triangle(whole):
    n = whole.shape[0]
    half = n // 2
    r = lax.broadcasted_iota(jnp.int32, (half, n), 0)
    c = lax.broadcasted_iota(jnp.int32, (half, n), 1)
    top, bottom = whole[:half], whole[half:]
    packed = jnp.where(c - half <= r, bottom, pltpu.roll(top, half, 1))
    diagonal = jnp.sum(jnp.where(r == c, top, 0.0), axis=0, keepdims=True)
    return packed, jnp.broadcast_to(diagonal, (8, n))


def symmetric(packed):
    n = packed.shape[1]
    half = n // 2
    r = lax.broadcasted_iota(jnp.int32, (half, n), 0)
    c = lax.broadcasted_iota(jnp.int32, (half, n), 1)
    rows, diagonal = packed[:half], packed[half : half + 1]
    top = jnp.where((c > r) & (c < half), pltpu.roll(rows, half, 1), 0.0)
    top = jnp.where(r == c, jnp.broadcast_to(diagonal, (half, n)), top)
    one = jnp.concatenate([top, jnp.where(c - half <= r, rows, 0.0)], axis=0)
    r = lax.broadcasted_iota(jnp.int32, (n, n), 0)
    c = lax.broadcasted_iota(jnp.int32, (n, n), 1)
    return jnp.where(r == c, one, one + one.T)


def outer_kernel(near, far1, far2, parts, mx_ref, gram_ref, out, total_ref, *rest):
    taken, halos, done, part_sems, halo_sems, out_sems = rest
    _, comps, _, cells_y, snaps, cells_z = halos.shape
    half = cells_y // 2
    width = cells_y * cells_z
    cells_x = mx_ref.shape[0]
    odd = lax.rem(lax.axis_index("stream"), 2)

    def part_read(e):
        return pltpu.make_async_copy(parts.at[e], taken.at[e], part_sems.at[e])

    def halo_reads(side, run):
        sem = halo_sems.at[side]
        is_near = (odd == 1) == (side == 0)
        first, second = pl.ds(0, half), pl.ds(half, half)

        @pl.when(is_near)
        def _():
            run(pltpu.make_async_copy(near, halos.at[side], sem.at[0]))

        @pl.when(jnp.logical_not(is_near))
        def _():
            run(pltpu.make_async_copy(far1, halos.at[side, :, :, first], sem.at[0]))
            run(pltpu.make_async_copy(far2, halos.at[side, :, :, second], sem.at[1]))

    for side in range(2):
        halo_reads(side, lambda copy: copy.start())
        for e in (2 * side, 2 * side + 1):
            part_read(e).start()
    total = gram_ref[...]
    writes = []
    last = cells_x - 1
    plan = (
        (0, 0, 0, (1.0, -8.0)),
        (1, 1, 0, (0.0, 1.0)),
        (2, last - 1, 1, (-1.0, 0.0)),
        (3, last, 1, (8.0, -1.0)),
    )
    for e, x, side, weights in plan:
        if e % 2 == 0:
            halo_reads(side, lambda copy: copy.wait())
        part_read(e).wait()
        metric_x = mx_ref[x]

        def some_rows(step, _):
            at = pl.ds(pl.multiple_of(step * ROWS, ROWS), ROWS)
            for f, (comp, sign) in enumerate(((2, -1.0), (1, 1.0), (0, 1.0))):
                for y in range(cells_y):
                    lanes = slice(f * width + y * cells_z, f * width + (y + 1) * cells_z)
                    sums = [
                        (sign * w) * halos[side, comp, k, y, at, :].astype(F32)
                        for k, w in enumerate(weights)
                        if w
                    ]
                    value = taken[e, at, lanes] + functools.reduce(jnp.add, sums) * metric_x
                    done[e, at, lanes] = value.astype(BF16)
            return 0

        lax.fori_loop(0, snaps // ROWS, some_rows, 0)
        writes.append(pltpu.make_async_copy(done.at[e], out.at[e], out_sems.at[e]))
        writes[-1].start()
        total += lax.dot_general(
            done[e], done[e], (((1,), (1,)), ((), ())), preferred_element_type=F32
        )
    half = snaps // 2
    total_ref[:half], total_ref[half:] = triangle(total)
    for w in writes:
        w.wait()


def outer_fields(metric_x, gram, parts, near, far1, far2):
    comps, _, cells_y, snaps, cells_z = near.shape
    lanes = parts.shape[2]
    return pl.pallas_call(
        outer_kernel,
        in_specs=[HBM] * 4 + [SMEM, VMEM],
        out_specs=[HBM, VMEM],
        out_shape=[
            jax.ShapeDtypeStruct(parts.shape, BF16),
            jax.ShapeDtypeStruct((snaps // 2 + 8, snaps), F32),
        ],
        scratch_shapes=[
            pltpu.VMEM(parts.shape, F32),
            pltpu.VMEM((2, comps, 2, cells_y, snaps, cells_z), BF16),
            pltpu.VMEM(parts.shape, BF16),
            DMA((4,)),
            DMA((2, 2)),
            DMA((4,)),
        ],
        compiler_params=limit(20),
    )(near, far1, far2, parts, metric_x, gram)


def factorize(rows, panel):
    eight, n = rows[0].shape
    shape = (eight, n)
    sub = lax.broadcasted_iota(jnp.int32, shape, 0)
    lane = lax.broadcasted_iota(jnp.int32, shape, 1)
    rows = list(rows)
    eyes = [jnp.where(lane == sub + eight * j, 1.0, 0.0).astype(F32) for j in range(len(rows))]
    uppers, inverses = [], []

    def spread(block, r):
        return jnp.broadcast_to(block[r : r + 1], shape)

    def join(parts):
        out = parts[0]
        for r in range(1, eight):
            out = jnp.where(sub == r, parts[r], out)
        return out

    for first in range(0, len(rows), panel):
        rest = first + panel
        for j in range(first, rest):
            at = eight * j
            left = {
                (r, c): jnp.broadcast_to(rows[j][r : r + 1, at + c : at + c + 1], shape)
                for r in range(eight)
                for c in range(r + 1)
            }
            upper = [spread(rows[j], r) for r in range(eight)]
            inverse = [spread(eyes[j], r) for r in range(eight)]
            for c in range(eight):
                root = lax.rsqrt(left[c, c])
                column = {r: left[r, c] * root for r in range(c + 1, eight)}
                for k in range(c + 1, eight):
                    for r in range(k, eight):
                        left[r, k] = left[r, k] - column[r] * column[k]
                upper[c] = upper[c] * root
                inverse[c] = inverse[c] * root
                for r in range(c + 1, eight):
                    upper[r] = upper[r] - column[r] * upper[c]
                    inverse[r] = inverse[r] - column[r] * inverse[c]
            for k in range(j + 1, rest):
                own = lane == sub + eight * k
                turned = [
                    jnp.sum(jnp.where(own, u, 0.0), axis=1, keepdims=True) for u in upper
                ]
                rows[k] = rows[k] - sum(t * u for t, u in zip(turned, upper))
                eyes[k] = eyes[k] - sum(t * v for t, v in zip(turned, inverse))
            uppers.append(join(upper))
            inverses.append(join(inverse))
        if rest < len(rows):
            u = jnp.concatenate(uppers[first:rest], axis=0)
            v = jnp.concatenate(inverses[first:rest], axis=0)
            below = u.T[eight * rest :]
            dot = functools.partial(
                jnp.dot, precision=lax.Precision.HIGHEST, preferred_element_type=F32
            )
            du, dv = dot(below, u), dot(below, v)
            for k in range(rest, len(rows)):
                o = slice(eight * (k - rest), eight * (k - rest + 1))
                rows[k] = rows[k] - du[o]
                eyes[k] = eyes[k] - dv[o]
    return jnp.concatenate(uppers, axis=0), jnp.concatenate(inverses, axis=0)


def modes_kernel(places, scale, n_terms, *rest):
    terms, rest = rest[:n_terms], rest[n_terms:]
    n = len(rest) - 7
    sources, (out, lower_ref, held, made, rows, in_sems, out_sems) = rest[:n], rest[n:]
    snaps, comps, _, cells_y, cells_z = out.shape
    width = cells_y * cells_z

    def reads(x):
        copies, lane = [], 0
        for m, (source, layer, count) in enumerate(places[x]):
            lanes = pl.ds(lane, count * width)
            lane += count * width
            copies.append(
                pltpu.make_async_copy(
                    sources[source].at[layer], held.at[x, :, lanes], in_sems.at[x, m]
                )
            )
        return copies

    for x in range(len(places)):
        for copy in reads(x):
            copy.start()

    gram = symmetric(tree_sum([term[...] for term in terms]) * scale)
    upper, inverse = factorize([gram[r : r + 8] for r in range(0, snaps, 8)], 8)
    r = lax.broadcasted_iota(jnp.int32, (snaps, snaps), 0)
    c = lax.broadcasted_iota(jnp.int32, (snaps, snaps), 1)
    lower_ref[...] = jnp.where(r >= c, upper.T, 0.0)
    inverse = inverse.astype(BF16)

    writes = []
    for x in range(len(places)):
        for copy in reads(x):
            copy.wait()
        for f in range(comps):
            lanes = slice(f * width, (f + 1) * width)
            whole = jnp.dot(inverse, held[x, :, lanes], preferred_element_type=F32)
            for y in range(cells_y):
                rows[f % 2, pl.ds(y, snaps, stride=PITCH), :] = whole[
                    :, y * cells_z : (y + 1) * cells_z
                ]
            for s in range(snaps):
                made[x, s, f] = rows[f % 2, pl.ds(s * PITCH, cells_y), :].astype(BF16)
        writes.append(pltpu.make_async_copy(made.at[x], out.at[:, :, x], out_sems.at[x]))
        writes[-1].start()
    for w in writes:
        w.wait()


def modes(terms, scale, sources, places, cells_y, cells_z):
    snaps = terms[0].shape[1]
    cells_x = len(places)
    return pl.pallas_call(
        functools.partial(modes_kernel, places, scale, len(terms)),
        in_specs=[VMEM] * len(terms) + [HBM] * len(sources),
        out_specs=[HBM, VMEM],
        out_shape=[
            jax.ShapeDtypeStruct((snaps, 4, cells_x, cells_y, cells_z), BF16),
            jax.ShapeDtypeStruct((snaps, snaps), F32),
        ],
        scratch_shapes=[
            pltpu.VMEM((cells_x, snaps, 4 * cells_y * cells_z), BF16),
            pltpu.VMEM((cells_x, snaps, 4, cells_y, cells_z), BF16),
            pltpu.VMEM((2, snaps * PITCH, cells_z), F32),
            DMA((cells_x, 2)),
            DMA((cells_x,)),
        ],
        compiler_params=limit(32),
    )(*terms, *sources)


def tree_sum(terms):
    while len(terms) > 1:
        terms = [terms[i] + terms[i + 1] for i in range(0, len(terms), 2)]
    return terms[0]


def exchange(local):
    groups = []
    for axis in ("cross", "stream"):
        count = lax.axis_size(axis)
        bits = [1 << k for k in range((count - 1).bit_length())]
        if axis == "cross":
            groups, bits = groups + [(axis, count, bits[:1])], bits[1:]
        groups += [(axis, count, bits[k : k + 2]) for k in range(0, len(bits), 2)]
    terms = [local]
    for axis, count, bits in groups:
        local = tree_sum(terms)
        steps = [sum(b for k, b in enumerate(bits) if n >> k & 1) for n in range(1 << len(bits))]
        terms = [local] + [
            lax.ppermute(local, axis, [(i, i ^ step) for i in range(count)]) for step in steps[1:]
        ]
    return terms


def shift(cells, axis, way):
    count = lax.axis_size(axis)
    pairs = [(i, i + way) for i in range(count) if 0 <= i + way < count]
    return lax.ppermute(cells, axis, pairs)


def both_ways(pairs):
    return [p for a, b in pairs for p in ((a, b), (b, a))]


def far_exchange(far2):
    count = lax.axis_size("stream")
    direct = both_ways([(i, i + 1) for i in range(1, count - 1, 2)])
    if count == 4:
        half_way = lax.ppermute(far2, "stream", [(1, 3), (2, 0)])
        return half_way, lambda cells: lax.ppermute(cells, "stream", [(3, 2), (0, 1)]), direct
    return far2, lambda cells: lax.ppermute(cells, "stream", direct), direct


def shards(velocity, metric_x, metric_y, metric_z):
    snaps, comps, cells_x, cells_y, cells_z = velocity.shape
    count = lax.axis_size("stream")
    near, far1, far2, first, last = edges(velocity)
    after_edges, _ = lax.optimization_barrier((velocity, near))
    half_way, second_hop, direct = far_exchange(far2)
    near = lax.ppermute(near, "stream", both_ways([(i, i + 1) for i in range(0, count - 1, 2)]))
    far1 = lax.ppermute(far1, "stream", direct)
    low = shift(last, "cross", 1)
    high = shift(first, "cross", -1)
    cells = planes(after_edges)
    half_way, cells = lax.optimization_barrier((half_way, cells))
    far2 = second_hop(half_way)

    taps = jnp.zeros((cells_z, cells_z), F32)
    for step, weight in ((1, 8.0), (-1, -8.0), (2, -1.0), (-2, 1.0)):
        taps = taps + weight * jnp.eye(cells_z, k=-step, dtype=F32)
    metrics = (metric_x / 12.0, metric_y / 12.0, metric_z[None, :] / 12.0, taps.astype(BF16))
    middle, ends, parts, gram = inner_fields(cells, low, high, metrics)
    outer, gram = outer_fields(metrics[0], gram, parts, near, far1, far2)
    everywhere = (
        4.0 * cells_x * lax.axis_size("stream") * cells_y * lax.axis_size("cross") * cells_z
    )
    terms = exchange(gram)
    end = lambda x: x if x < 2 else x - cells_x + 4
    places = [
        [(0, x - 2, 4)] if 2 <= x < cells_x - 2 else [(1, end(x), 1), (2, end(x), 3)]
        for x in range(cells_x)
    ]
    sources = [middle, ends, outer]
    return tuple(modes(terms, 1.0 / everywhere, sources, places, cells_y, cells_z))


def solution(mesh):
    return jax.shard_map(
        shards,
        mesh=mesh,
        in_specs=(P(None, None, "stream", "cross", None), P("stream"), P("cross"), P()),
        out_specs=(P(None, None, "stream", "cross", None), P()),
        check_vma=False,
    )
```

```python
import functools

import jax
import jax.numpy as jnp
from jax import lax
from jax.experimental import pallas as pl
from jax.experimental.pallas import tpu as pltpu
from jax.sharding import PartitionSpec as P

F32, BF16 = jnp.float32, jnp.bfloat16
PITCH = 9
ROWS = 16
SLOTS = 4
HBM = pl.BlockSpec(memory_space=pl.ANY)
SMEM = pl.BlockSpec(memory_space=pltpu.SMEM)
VMEM = pl.BlockSpec(memory_space=pltpu.VMEM)
DMA = pltpu.SemaphoreType.DMA


def limit(mib):
    return pltpu.CompilerParams(vmem_limit_bytes=mib * 1024 * 1024)


def turn(tile, rows, ys, put):
    snaps, cells_y, cells_z = tile.shape
    wide = tile.astype(F32)
    for s in range(snaps):
        rows[pl.ds(s * PITCH, cells_y), :] = wide[s]
    for y in ys:
        put(y, rows[pl.ds(y, snaps, stride=PITCH), :].astype(BF16))


def edges_kernel(
    velocity, near, far1, far2, first, last, tiles, inner, ends, sides, rows, *sems
):
    end_in, inner_in, end_out, side_out = sems
    snaps, comps, cells_x, cells_y, _ = velocity.shape
    odd = lax.rem(lax.axis_index("stream"), 2)
    firsts = ((1 - odd) * (cells_x - 2), odd * (cells_x - 2))
    half = cells_y // 2
    between = cells_x - 4
    order = [(side, c) for side in (1, 0) for c in range(comps)]

    def end_read(side, c):
        return pltpu.make_async_copy(
            velocity.at[:, c, pl.ds(firsts[side], 2)], tiles.at[side, c], end_in.at[side, c]
        )

    def inner_read(c):
        return pltpu.make_async_copy(
            velocity.at[:, c, pl.ds(2, between)], inner.at[c], inner_in.at[c]
        )

    def side_writes(c):
        return [
            pltpu.make_async_copy(sides.at[k, c], ref.at[c], side_out.at[k, c])
            for k, ref in enumerate((first, last))
        ]

    def put_side(c, x, y, plane):
        if y < 2:
            sides[0, c, x, y] = plane
        elif y >= cells_y - 2:
            sides[1, c, x, y - cells_y + 2] = plane

    for side, c in order:
        end_read(side, c).start()
    for c in range(comps):
        inner_read(c).start()
    writes = []
    for side, c in order:
        end_read(side, c).wait()

        def one_end(layer, _):
            x = firsts[side] + layer

            def put(y, plane):
                ends[side, c, layer, y] = plane
                put_side(c, x, y, plane)

            turn(tiles[side, c, :, layer], rows, range(cells_y), put)
            return 0

        lax.fori_loop(0, 2, one_end, 0)
        if side == 0:
            parts = [(ends.at[0, c], near.at[c])]
        else:
            parts = [
                (ends.at[1, c, :, pl.ds(0, half)], far1.at[c]),
                (ends.at[1, c, :, pl.ds(half, half)], far2.at[c]),
            ]
        for src, dst in parts:
            writes.append(pltpu.make_async_copy(src, dst, end_out.at[len(writes)]))
            writes[-1].start()

    for c in range(comps):
        inner_read(c).wait()

        def one_inner(n, _):
            turn(
                inner[c, :, n],
                rows,
                (0, 1, cells_y - 2, cells_y - 1),
                functools.partial(put_side, c, n + 2),
            )
            return 0

        lax.fori_loop(0, between, one_inner, 0)
        for w in side_writes(c):
            w.start()

    for w in writes:
        w.wait()
    for c in range(comps):
        for w in side_writes(c):
            w.wait()


def edges(velocity):
    snaps, comps, cells_x, cells_y, cells_z = velocity.shape
    shape = lambda layers, rows: jax.ShapeDtypeStruct((comps, layers, rows, snaps, cells_z), BF16)
    return pl.pallas_call(
        edges_kernel,
        in_specs=[HBM],
        out_specs=[HBM] * 5,
        out_shape=[shape(2, cells_y)] + [shape(2, cells_y // 2)] * 2 + [shape(cells_x, 2)] * 2,
        scratch_shapes=[
            pltpu.VMEM((2, comps, snaps, 2, cells_y, cells_z), BF16),
            pltpu.VMEM((comps, snaps, cells_x - 4, cells_y, cells_z), BF16),
            pltpu.VMEM((2, comps, 2, cells_y, snaps, cells_z), BF16),
            pltpu.VMEM((2, comps, cells_x, 2, snaps, cells_z), BF16),
            pltpu.VMEM((snaps * PITCH, cells_z), F32),
            DMA((2, comps)),
            DMA((comps,)),
            DMA((3 * comps,)),
            DMA((2, comps)),
        ],
        compiler_params=limit(60),
    )(velocity)


def planes_kernel(velocity, cells, taken, turned, rows, in_sems, out_sems):
    snaps, comps, cells_x, cells_y, cells_z = velocity.shape

    def read(c, x):
        return pltpu.make_async_copy(velocity.at[:, c, x], taken.at[c, x], in_sems.at[c, x])

    def write(c, x):
        return pltpu.make_async_copy(turned.at[c, x], cells.at[c, x], out_sems.at[c, x])

    def each(work):
        def step(n, _):
            work(n // cells_x, lax.rem(n, cells_x))
            return 0

        lax.fori_loop(0, comps * cells_x, step, 0)

    def one(c, x):
        read(c, x).wait()

        def put(y, plane):
            turned[c, x, y] = plane

        turn(taken[c, x], rows, range(cells_y), put)
        write(c, x).start()

    each(lambda c, x: read(c, x).start())
    each(one)
    each(lambda c, x: write(c, x).wait())


def planes(velocity):
    snaps, comps, cells_x, cells_y, cells_z = velocity.shape
    return pl.pallas_call(
        planes_kernel,
        in_specs=[HBM],
        out_specs=HBM,
        out_shape=jax.ShapeDtypeStruct((comps, cells_x, cells_y, snaps, cells_z), BF16),
        scratch_shapes=[
            pltpu.VMEM((comps, cells_x, snaps, cells_y, cells_z), BF16),
            pltpu.VMEM((comps, cells_x, cells_y, snaps, cells_z), BF16),
            pltpu.VMEM((snaps * PITCH, cells_z), F32),
            DMA((comps, cells_x)),
            DMA((comps, cells_x)),
        ],
        compiler_params=limit(60),
    )(velocity)


def layer_fields(ring, slots, rz, low, high, metric_x, metric_y_ref, metric_z, puts):
    cells_y, snaps, cells_z = ring.shape[2:]
    back2, back1, here, fore1, fore2 = slots

    def some_rows(step, _):
        at = pl.ds(pl.multiple_of(step * ROWS, ROWS), ROWS)

        def row(comp, y):
            if y < 0:
                return low[comp, y + 2, at, :].astype(F32)
            if y >= cells_y:
                return high[comp, y - cells_y, at, :].astype(F32)
            return ring[here, comp, y, at, :]

        window = [[row(c, y) for y in range(-2, 2)] for c in range(3)]
        for y in range(cells_y):
            for c in range(3):
                window[c].append(row(c, y + 2))

            def along_x(c):
                near = ring[fore1, c, y, at, :] - ring[back1, c, y, at, :]
                far = ring[fore2, c, y, at, :] - ring[back2, c, y, at, :]
                return (8.0 * near - far) * metric_x

            def along_y(c):
                w = window[c]
                return (8.0 * (w[3] - w[1]) - (w[4] - w[0])) * metric_y_ref[y]

            def along_z(c):
                return rz[c, y, at, :] * metric_z

            puts[0](at, y, along_y(2) - along_z(1))
            puts[1](at, y, along_z(0) - along_x(2))
            puts[2](at, y, along_x(1) - along_y(0))
            puts[3](at, y, along_x(0) + along_y(1) + along_z(2))
            for c in range(3):
                window[c] = window[c][1:]
        return 0

    lax.fori_loop(0, snaps // ROWS, some_rows, 0, unroll=2)


def inner_kernel(mx_ref, my_ref, mz_ref, taps_ref, cells, low, high, *rest):
    middle, ends, parts, gram_ref = rest[:4]
    layers, lows, highs, ring, rz_ring, done, done_ends, done_parts, in_sems, out_sems = rest[4:]
    comps, cells_y, snaps, cells_z = ring.shape[1:]
    cells_x = lows.shape[0]
    width = cells_y * cells_z

    def reads(x):
        return [
            pltpu.make_async_copy(cells.at[:, x], layers.at[x % SLOTS], in_sems.at[0, x]),
            pltpu.make_async_copy(low.at[:, x], lows.at[x], in_sems.at[1, x]),
            pltpu.make_async_copy(high.at[:, x], highs.at[x], in_sems.at[2, x]),
        ]

    def put_in(ref, lane):
        def put(at, y, value):
            ref[at, lane + y * cells_z : lane + (y + 1) * cells_z] = value.astype(ref.dtype)

        return put

    for x in range(SLOTS):
        for copy in reads(x):
            copy.start()
    gram_ref[...] = jnp.zeros_like(gram_ref)
    writes, middle_writes = [], []

    def write(src, dst):
        sem = out_sems.at[len(writes) + len(middle_writes)]
        writes.append(pltpu.make_async_copy(src, dst, sem))
        writes[-1].start()

    for i in range(cells_x + 4):
        if 2 <= i < cells_x + 2:
            for copy in reads(i - 2):
                copy.wait()
            slot = layers.at[(i - 2) % SLOTS]
            ring[i % 5] = slot[...].astype(F32)
            flat = slot[...].reshape(comps * cells_y * snaps, cells_z)
            rz_ring[i % 3] = jnp.dot(flat, taps_ref[...], preferred_element_type=F32).reshape(
                comps, cells_y, snaps, cells_z
            )
            if i - 2 + SLOTS < cells_x:
                for copy in reads(i - 2 + SLOTS):
                    copy.start()
        else:
            ring[i % 5] = jnp.zeros(ring.shape[1:], F32)
        x = i - 4
        if x < 0:
            continue
        is_inner = 2 <= x < cells_x - 2
        e = x if x < 2 else x - cells_x + 4
        if is_inner:
            made = done.at[x % SLOTS]
            if x - 2 >= SLOTS:
                middle_writes[x - 2 - SLOTS].wait()
            puts = [put_in(made, f * width) for f in range(4)]
        else:
            made = done_ends.at[e]
            puts = [put_in(made, 0)]
            puts += [put_in(done_parts.at[e], f * width) for f in range(3)]
        layer_fields(
            ring,
            [(i + 1 + s) % 5 for s in range(5)],
            rz_ring.at[(i - 2) % 3],
            lows.at[x],
            highs.at[x],
            mx_ref[x],
            my_ref,
            mz_ref[...],
            puts,
        )
        if is_inner:
            write(made, middle.at[x - 2])
            middle_writes.append(writes.pop())
        else:
            write(made, ends.at[e])
            write(done_parts.at[e], parts.at[e])
        gram_ref[...] += lax.dot_general(
            made[...], made[...], (((1,), (1,)), ((), ())), preferred_element_type=F32
        )
    for w in writes + middle_writes[-SLOTS:]:
        w.wait()


def inner_fields(cells, low, high, metrics):
    comps, cells_x, cells_y, snaps, cells_z = cells.shape
    width = cells_y * cells_z
    return pl.pallas_call(
        inner_kernel,
        in_specs=[SMEM, SMEM, VMEM, VMEM] + [HBM] * 3,
        out_specs=[HBM] * 3 + [VMEM],
        out_shape=[
            jax.ShapeDtypeStruct((cells_x - 4, snaps, 4 * width), BF16),
            jax.ShapeDtypeStruct((4, snaps, width), BF16),
            jax.ShapeDtypeStruct((4, snaps, 3 * width), F32),
            jax.ShapeDtypeStruct((snaps, snaps), F32),
        ],
        scratch_shapes=[
            pltpu.VMEM((SLOTS, comps, cells_y, snaps, cells_z), BF16),
            pltpu.VMEM((cells_x, comps, 2, snaps, cells_z), BF16),
            pltpu.VMEM((cells_x, comps, 2, snaps, cells_z), BF16),
            pltpu.VMEM((5, comps, cells_y, snaps, cells_z), F32),
            pltpu.VMEM((3, comps, cells_y, snaps, cells_z), F32),
            pltpu.VMEM((SLOTS, snaps, 4 * width), BF16),
            pltpu.VMEM((4, snaps, width), BF16),
            pltpu.VMEM((4, snaps, 3 * width), F32),
            DMA((3, cells_x)),
            DMA((cells_x + 4,)),
        ],
        compiler_params=limit(36),
    )(*metrics, cells, low, high)


def triangle(whole):
    n = whole.shape[0]
    half = n // 2
    r = lax.broadcasted_iota(jnp.int32, (half, n), 0)
    c = lax.broadcasted_iota(jnp.int32, (half, n), 1)
    top, bottom = whole[:half], whole[half:]
    packed = jnp.where(c - half <= r, bottom, pltpu.roll(top, half, 1))
    diagonal = jnp.sum(jnp.where(r == c, top, 0.0), axis=0, keepdims=True)
    return packed, jnp.broadcast_to(diagonal, (8, n))


def symmetric(packed):
    n = packed.shape[1]
    half = n // 2
    r = lax.broadcasted_iota(jnp.int32, (half, n), 0)
    c = lax.broadcasted_iota(jnp.int32, (half, n), 1)
    rows, diagonal = packed[:half], packed[half : half + 1]
    top = jnp.where((c > r) & (c < half), pltpu.roll(rows, half, 1), 0.0)
    top = jnp.where(r == c, jnp.broadcast_to(diagonal, (half, n)), top)
    one = jnp.concatenate([top, jnp.where(c - half <= r, rows, 0.0)], axis=0)
    r = lax.broadcasted_iota(jnp.int32, (n, n), 0)
    c = lax.broadcasted_iota(jnp.int32, (n, n), 1)
    return jnp.where(r == c, one, one + one.T)


def outer_kernel(near, far1, far2, parts, mx_ref, gram_ref, out, total_ref, *rest):
    taken, halos, done, part_sems, halo_sems, out_sems = rest
    _, comps, _, cells_y, snaps, cells_z = halos.shape
    half = cells_y // 2
    width = cells_y * cells_z
    cells_x = mx_ref.shape[0]
    odd = lax.rem(lax.axis_index("stream"), 2)

    def part_read(e):
        return pltpu.make_async_copy(parts.at[e], taken.at[e], part_sems.at[e])

    def halo_reads(side, run):
        sem = halo_sems.at[side]
        is_near = (odd == 1) == (side == 0)
        first, second = pl.ds(0, half), pl.ds(half, half)

        @pl.when(is_near)
        def _():
            run(pltpu.make_async_copy(near, halos.at[side], sem.at[0]))

        @pl.when(jnp.logical_not(is_near))
        def _():
            run(pltpu.make_async_copy(far1, halos.at[side, :, :, first], sem.at[0]))
            run(pltpu.make_async_copy(far2, halos.at[side, :, :, second], sem.at[1]))

    for side in range(2):
        halo_reads(side, lambda copy: copy.start())
        for e in (2 * side, 2 * side + 1):
            part_read(e).start()
    total = gram_ref[...]
    writes = []
    last = cells_x - 1
    plan = (
        (0, 0, 0, (1.0, -8.0)),
        (1, 1, 0, (0.0, 1.0)),
        (2, last - 1, 1, (-1.0, 0.0)),
        (3, last, 1, (8.0, -1.0)),
    )
    for e, x, side, weights in plan:
        if e % 2 == 0:
            halo_reads(side, lambda copy: copy.wait())
        part_read(e).wait()
        metric_x = mx_ref[x]

        def some_rows(step, _):
            at = pl.ds(pl.multiple_of(step * ROWS, ROWS), ROWS)
            for f, (comp, sign) in enumerate(((2, -1.0), (1, 1.0), (0, 1.0))):
                for y in range(cells_y):
                    lanes = slice(f * width + y * cells_z, f * width + (y + 1) * cells_z)
                    sums = [
                        (sign * w) * halos[side, comp, k, y, at, :].astype(F32)
                        for k, w in enumerate(weights)
                        if w
                    ]
                    value = taken[e, at, lanes] + functools.reduce(jnp.add, sums) * metric_x
                    done[e, at, lanes] = value.astype(BF16)
            return 0

        lax.fori_loop(0, snaps // ROWS, some_rows, 0)
        writes.append(pltpu.make_async_copy(done.at[e], out.at[e], out_sems.at[e]))
        writes[-1].start()
        total += lax.dot_general(
            done[e], done[e], (((1,), (1,)), ((), ())), preferred_element_type=F32
        )
    half = snaps // 2
    total_ref[:half], total_ref[half:] = triangle(total)
    for w in writes:
        w.wait()


def outer_fields(metric_x, gram, parts, near, far1, far2):
    comps, _, cells_y, snaps, cells_z = near.shape
    lanes = parts.shape[2]
    return pl.pallas_call(
        outer_kernel,
        in_specs=[HBM] * 4 + [SMEM, VMEM],
        out_specs=[HBM, VMEM],
        out_shape=[
            jax.ShapeDtypeStruct(parts.shape, BF16),
            jax.ShapeDtypeStruct((snaps // 2 + 8, snaps), F32),
        ],
        scratch_shapes=[
            pltpu.VMEM(parts.shape, F32),
            pltpu.VMEM((2, comps, 2, cells_y, snaps, cells_z), BF16),
            pltpu.VMEM(parts.shape, BF16),
            DMA((4,)),
            DMA((2, 2)),
            DMA((4,)),
        ],
        compiler_params=limit(20),
    )(near, far1, far2, parts, metric_x, gram)


def factorize(rows, panel):
    eight, n = rows[0].shape
    shape = (eight, n)
    sub = lax.broadcasted_iota(jnp.int32, shape, 0)
    lane = lax.broadcasted_iota(jnp.int32, shape, 1)
    rows = list(rows)
    eyes = [jnp.where(lane == sub + eight * j, 1.0, 0.0).astype(F32) for j in range(len(rows))]
    uppers, inverses = [], []

    def spread(block, r):
        return jnp.broadcast_to(block[r : r + 1], shape)

    def join(parts):
        out = parts[0]
        for r in range(1, eight):
            out = jnp.where(sub == r, parts[r], out)
        return out

    for first in range(0, len(rows), panel):
        rest = first + panel
        for j in range(first, rest):
            at = eight * j
            left = {
                (r, c): jnp.broadcast_to(rows[j][r : r + 1, at + c : at + c + 1], shape)
                for r in range(eight)
                for c in range(r + 1)
            }
            upper = [spread(rows[j], r) for r in range(eight)]
            inverse = [spread(eyes[j], r) for r in range(eight)]
            for c in range(eight):
                root = lax.rsqrt(left[c, c])
                column = {r: left[r, c] * root for r in range(c + 1, eight)}
                for k in range(c + 1, eight):
                    for r in range(k, eight):
                        left[r, k] = left[r, k] - column[r] * column[k]
                upper[c] = upper[c] * root
                inverse[c] = inverse[c] * root
                for r in range(c + 1, eight):
                    upper[r] = upper[r] - column[r] * upper[c]
                    inverse[r] = inverse[r] - column[r] * inverse[c]
            for k in range(j + 1, rest):
                own = lane == sub + eight * k
                turned = [
                    jnp.sum(jnp.where(own, u, 0.0), axis=1, keepdims=True) for u in upper
                ]
                rows[k] = rows[k] - sum(t * u for t, u in zip(turned, upper))
                eyes[k] = eyes[k] - sum(t * v for t, v in zip(turned, inverse))
            uppers.append(join(upper))
            inverses.append(join(inverse))
        if rest < len(rows):
            u = jnp.concatenate(uppers[first:rest], axis=0)
            v = jnp.concatenate(inverses[first:rest], axis=0)
            below = u.T[eight * rest :]
            dot = functools.partial(
                jnp.dot, precision=lax.Precision.HIGHEST, preferred_element_type=F32
            )
            du, dv = dot(below, u), dot(below, v)
            for k in range(rest, len(rows)):
                o = slice(eight * (k - rest), eight * (k - rest + 1))
                rows[k] = rows[k] - du[o]
                eyes[k] = eyes[k] - dv[o]
    return jnp.concatenate(uppers, axis=0), jnp.concatenate(inverses, axis=0)


def modes_kernel(places, scale, n_terms, *rest):
    terms, rest = rest[:n_terms], rest[n_terms:]
    n = len(rest) - 7
    sources, (out, lower_ref, held, made, rows, in_sems, out_sems) = rest[:n], rest[n:]
    snaps, comps, _, cells_y, cells_z = out.shape
    width = cells_y * cells_z

    def reads(x):
        copies, lane = [], 0
        for m, (source, layer, count) in enumerate(places[x]):
            lanes = pl.ds(lane, count * width)
            lane += count * width
            copies.append(
                pltpu.make_async_copy(
                    sources[source].at[layer], held.at[x, :, lanes], in_sems.at[x, m]
                )
            )
        return copies

    for x in range(len(places)):
        for copy in reads(x):
            copy.start()

    gram = symmetric(tree_sum([term[...] for term in terms]) * scale)
    upper, inverse = factorize([gram[r : r + 8] for r in range(0, snaps, 8)], 8)
    r = lax.broadcasted_iota(jnp.int32, (snaps, snaps), 0)
    c = lax.broadcasted_iota(jnp.int32, (snaps, snaps), 1)
    lower_ref[...] = jnp.where(r >= c, upper.T, 0.0)
    inverse = inverse.astype(BF16)

    writes = []
    for x in range(len(places)):
        for copy in reads(x):
            copy.wait()
        for f in range(comps):
            lanes = slice(f * width, (f + 1) * width)
            whole = jnp.dot(inverse, held[x, :, lanes], preferred_element_type=F32)
            for y in range(cells_y):
                rows[f % 2, pl.ds(y, snaps, stride=PITCH), :] = whole[
                    :, y * cells_z : (y + 1) * cells_z
                ]
            for s in range(snaps):
                made[x, s, f] = rows[f % 2, pl.ds(s * PITCH, cells_y), :].astype(BF16)
        writes.append(pltpu.make_async_copy(made.at[x], out.at[:, :, x], out_sems.at[x]))
        writes[-1].start()
    for w in writes:
        w.wait()


def modes(terms, scale, sources, places, cells_y, cells_z):
    snaps = terms[0].shape[1]
    cells_x = len(places)
    return pl.pallas_call(
        functools.partial(modes_kernel, places, scale, len(terms)),
        in_specs=[VMEM] * len(terms) + [HBM] * len(sources),
        out_specs=[HBM, VMEM],
        out_shape=[
            jax.ShapeDtypeStruct((snaps, 4, cells_x, cells_y, cells_z), BF16),
            jax.ShapeDtypeStruct((snaps, snaps), F32),
        ],
        scratch_shapes=[
            pltpu.VMEM((cells_x, snaps, 4 * cells_y * cells_z), BF16),
            pltpu.VMEM((cells_x, snaps, 4, cells_y, cells_z), BF16),
            pltpu.VMEM((2, snaps * PITCH, cells_z), F32),
            DMA((cells_x, 2)),
            DMA((cells_x,)),
        ],
        compiler_params=limit(32),
    )(*terms, *sources)


def tree_sum(terms):
    while len(terms) > 1:
        terms = [terms[i] + terms[i + 1] for i in range(0, len(terms), 2)]
    return terms[0]


def exchange(local):
    groups = []
    for axis in ("cross", "stream"):
        count = lax.axis_size(axis)
        bits = [1 << k for k in range((count - 1).bit_length())]
        if axis == "cross":
            groups, bits = groups + [(axis, count, bits[:1])], bits[1:]
        groups += [(axis, count, bits[k : k + 2]) for k in range(0, len(bits), 2)]
    terms = [local]
    for axis, count, bits in groups:
        local = tree_sum(terms)
        steps = [sum(b for k, b in enumerate(bits) if n >> k & 1) for n in range(1 << len(bits))]
        terms = [local] + [
            lax.ppermute(local, axis, [(i, i ^ step) for i in range(count)]) for step in steps[1:]
        ]
    return terms


def shift(cells, axis, way):
    count = lax.axis_size(axis)
    pairs = [(i, i + way) for i in range(count) if 0 <= i + way < count]
    return lax.ppermute(cells, axis, pairs)


def both_ways(pairs):
    return [p for a, b in pairs for p in ((a, b), (b, a))]


def far_exchange(far2):
    count = lax.axis_size("stream")
    direct = both_ways([(i, i + 1) for i in range(1, count - 1, 2)])
    if count == 4:
        half_way = lax.ppermute(far2, "stream", [(1, 3), (2, 0)])
        return half_way, lambda cells: lax.ppermute(cells, "stream", [(3, 2), (0, 1)]), direct
    return far2, lambda cells: lax.ppermute(cells, "stream", direct), direct


def shards(velocity, metric_x, metric_y, metric_z):
    snaps, comps, cells_x, cells_y, cells_z = velocity.shape
    count = lax.axis_size("stream")
    near, far1, far2, first, last = edges(velocity)
    after_edges, _ = lax.optimization_barrier((velocity, near))
    half_way, second_hop, direct = far_exchange(far2)
    near = lax.ppermute(near, "stream", both_ways([(i, i + 1) for i in range(0, count - 1, 2)]))
    far1 = lax.ppermute(far1, "stream", direct)
    low = shift(last, "cross", 1)
    high = shift(first, "cross", -1)
    cells = planes(after_edges)
    half_way, cells = lax.optimization_barrier((half_way, cells))
    far2 = second_hop(half_way)

    taps = jnp.zeros((cells_z, cells_z), F32)
    for step, weight in ((1, 8.0), (-1, -8.0), (2, -1.0), (-2, 1.0)):
        taps = taps + weight * jnp.eye(cells_z, k=-step, dtype=F32)
    metrics = (metric_x / 12.0, metric_y / 12.0, metric_z[None, :] / 12.0, taps.astype(BF16))
    middle, ends, parts, gram = inner_fields(cells, low, high, metrics)
    outer, gram = outer_fields(metrics[0], gram, parts, near, far1, far2)
    everywhere = (
        4.0 * cells_x * lax.axis_size("stream") * cells_y * lax.axis_size("cross") * cells_z
    )
    terms = exchange(gram)
    end = lambda x: x if x < 2 else x - cells_x + 4
    places = [
        [(0, x - 2, 4)] if 2 <= x < cells_x - 2 else [(1, end(x), 1), (2, end(x), 3)]
        for x in range(cells_x)
    ]
    sources = [middle, ends, outer]
    return tuple(modes(terms, 1.0 / everywhere, sources, places, cells_y, cells_z))


def solution(mesh):
    return jax.shard_map(
        shards,
        mesh=mesh,
        in_specs=(P(None, None, "stream", "cross", None), P("stream"), P("cross"), P()),
        out_specs=(P(None, None, "stream", "cross", None), P()),
        check_vma=False,
    )
```
